32 devices in a mesh: pack: 8 (over z, x), seq: 4 (over y, core).
Axes of the slice: x: 2, y: 2, z: 4, core: 2. Of those that a mesh axis runs over, the one named last changes fastest.
Arguments:
- tokens: bfloat16 [16, 2304, 1152], P('pack', 'seq'), may hold values from -6 to 6
- condition: bfloat16 [16, 2304, 1152], P('pack', 'seq'), may hold values from -6 to 6
- image_ids: int32 [16, 2304], P('pack', 'seq'), may hold values from 0 to 8, as said below
- ada_weight: bfloat16 [1152, 6912], P('pack', 'seq'), may hold values from -0.1875 to 0.1875
- attn_weight: bfloat16 [1152, 3456], P('pack', 'seq'), may hold values from -0.1875 to 0.1875
- out_weight: bfloat16 [1152, 1152], P('pack', 'seq'), may hold values from -0.75 to 0.75
- up_weight: bfloat16 [1152, 4608], P('pack', 'seq'), may hold values from -0.1875 to 0.1875
- down_weight: bfloat16 [4608, 1152], P('pack', 'seq'), may hold values from -0.09375 to 0.09375
- biases: bfloat16 [16128], P(('pack', 'seq')), may hold values from -1.5 to 1.5
- cotangent: bfloat16 [16, 2304, 1152], P('pack', 'seq'), may hold values from -6 to 6
Outputs:
- block_out: bfloat16 [16, 2304, 1152], P('pack', 'seq')
- tokens_grad: float32 [16, 2304, 1152], P('pack', 'seq')
- condition_grad: float32 [16, 2304, 1152], P('pack', 'seq')
- ada_grad: float32 [1152, 6912], P('pack', 'seq')
- attn_grad: float32 [1152, 3456], P('pack', 'seq')
- out_grad: float32 [1152, 1152], P('pack', 'seq')
- up_grad: float32 [1152, 4608], P('pack', 'seq')
- down_grad: float32 [4608, 1152], P('pack', 'seq')
- bias_grad: float32 [16128], P(('pack', 'seq'))
The draws below stay inside these ranges and needn't reach their ends.
Inputs may be any that keep to these rules, and one draw needn't show every extreme that they name: `image_ids`: in each row the image numbers start at 0, never fall and rise by at most one from a position to the next; in each aligned block of 2 rows one row holds a single image and the other holds 9 images.
All inputs are finite; a program needn't handle non-finite values.
Results may differ from the reference program's by a relative error of at most 0.014.
The reference program's roundings to bfloat16 on the way count: a program that leaves them out, or rounds other values in their place, can miss the bound.
Values may be sent and summed in bfloat16 or wider, within the bound.
No kernel may reach another device: no remote copies, remote signals or barrier semaphores. Data moves between devices by JAX's collectives and lax.ppermute only.
A program may use at most 576 MiB of HBM per device.

```python
import jax
import jax.numpy as jnp
from jax import lax

D = 1152
HEADS = 16
HD = 72
FF = 4608
LEN = 2304
ROWS_DEV = 2
ROWS = 16
NB = 16128


def draw_image_ids(key, part):
    offset_key, flag_key, row_key = jax.random.split(key, 3)
    pieces = max(2, LEN // 256)
    segment = LEN // pieces
    reach = segment // 4
    offsets = jax.random.randint(offset_key, (ROWS, pieces - 1), -reach, reach + 1)
    cuts = (jnp.arange(1, pieces, dtype=jnp.int32) * segment)[None, :] + offsets
    flags = jax.random.randint(flag_key, (ROWS, pieces - 1), 0, 2) == 1
    chosen = jnp.repeat(jax.random.randint(row_key, (ROWS // ROWS_DEV,), 0, ROWS_DEV), ROWS_DEV)
    within = jnp.arange(ROWS) % ROWS_DEV
    whole_row = within == chosen
    full_row = within == (chosen + 1) % ROWS_DEV
    flags = jnp.where(full_row[:, None], True, flags)
    flags = jnp.where(whole_row[:, None], False, flags)
    places = jnp.arange(LEN, dtype=jnp.int32)
    passed = (places[None, :, None] >= cuts[:, None, :]) & flags[:, None, :]
    return jnp.sum(passed.astype(jnp.int32), axis=2).astype(jnp.int32)


def raised(values, own_key, source, target, shards_of, factor):
    owner, partner = [(jnp.arange(values.shape[axis_at]) // (values.shape[axis_at] // shards_of)).reshape([-1 if axis == axis_at else 1 for axis in range(values.ndim)]) for axis_at in (source, target)]
    chosen = jax.random.permutation(own_key, shards_of)[partner]
    strong = (owner == chosen) | (owner == (partner + shards_of // 2) % shards_of)
    return jnp.where(strong, factor * values, values)


def block_scale(stream_key, shape, cuts, smallest, top_value):
    level, own = 1.0, jax.random.fold_in(stream_key, 6)
    for axis_at, shards_of in cuts:
        steps = jnp.exp(jax.random.uniform(jax.random.fold_in(own, axis_at), (shards_of,), jnp.float32, smallest / len(cuts), top_value / len(cuts)))
        level = level * jnp.repeat(steps, shape[axis_at] // shards_of).reshape([-1 if axis == axis_at else 1 for axis in range(len(shape))])
    return level


def normal_values(key, dims, deviation, most, cuts=(), held_as=jnp.bfloat16):
    array = jax.random.normal(key, dims, jnp.float32) * deviation
    if len(cuts) > 0:
        array = block_scale(key, dims, cuts, -0.22, 0.18) * array
    return jnp.clip(array, min=-most, max=most).astype(held_as)


def gaussian_with(own_key, shape, deviation, bound, cuts, heavy, kind=jnp.bfloat16):
    array = deviation * jax.random.normal(own_key, shape, jnp.float32)
    if cuts:
        array = array * block_scale(own_key, shape, cuts, -0.22, 0.18)
    return jnp.clip(raised(array, jax.random.fold_in(own_key, 3), *heavy), -bound, bound).astype(kind)


def setup_inputs(seed: int = 0) -> dict:
    key_of = jax.random.split(jax.random.key(seed), 11)
    tokens = gaussian_with(key_of[0], (ROWS, LEN, D), 1.0, 6.0, ((0, 8), (1, 4)), (0, 2, 8, 2.0))
    condition = normal_values(key_of[1], (ROWS, LEN, D), 1.0, 6.0, ((0, 8), (1, 4)))
    image_ids = draw_image_ids(jax.random.fold_in(key_of[10], 71), 0)
    ada_weight = normal_values(key_of[3], (D, 6 * D), D ** -0.5, 0.1875, ((0, 8), (1, 4)))
    attn_weight = normal_values(key_of[4], (D, 3 * D), D ** -0.5, 0.1875, ((0, 8), (1, 4)))
    out_weight = normal_values(key_of[5], (D, D), (D // 16) ** -0.5, 0.75, ((0, 8), (1, 4)))
    up_weight = normal_values(key_of[6], (D, FF), D ** -0.5, 0.1875, ((0, 8), (1, 4)))
    down_weight = normal_values(key_of[7], (FF, D), FF ** -0.5, 0.09375, ((0, 8), (1, 4)))
    biases = normal_values(key_of[8], (NB,), 0.3, 1.5, ((0, 32),))
    cotangent = gaussian_with(key_of[9], (ROWS, LEN, D), 1.0, 6.0, ((0, 8), (1, 4)), (1, 2, 4, 2.0))
    return {"tokens": tokens, "condition": condition, "image_ids": image_ids, "ada_weight": ada_weight, "attn_weight": attn_weight, "out_weight": out_weight, "up_weight": up_weight, "down_weight": down_weight, "biases": biases, "cotangent": cotangent}


@jax.custom_vjp
def low(v):
    return lax.optimization_barrier(v.astype(jnp.bfloat16)).astype(jnp.float32)

@jax.custom_vjp
def low_back(v):
    return v

def low_keep(v):
    return (low(v), None)

def low_pass(kept, grad):
    return (grad,)

def back_keep(v):
    return (v, None)

def back_low(kept, grad):
    return (low(grad),)
low.defvjp(low_keep, low_pass)
low_back.defvjp(back_keep, back_low)
EPS = 1e-06

def modulate(values, shift_by, scale_by):
    center = values - lax.optimization_barrier(jnp.mean(values, axis=-1, keepdims=True))
    spread = lax.optimization_barrier(jnp.mean(center * center, axis=-1, keepdims=True))
    return center * lax.rsqrt(spread + EPS) * (1.0 + scale_by) + shift_by

def dense(inputs, weight, offset):
    return jnp.dot(inputs, weight, precision=lax.Precision.HIGHEST, preferred_element_type=jnp.float32) + offset

def to_heads(values):
    return values.reshape(values.shape[0], HEADS, HD).transpose(1, 0, 2)

def attend(queries, key_rows, value_rows, image_row):
    same_image = image_row[:, None] == image_row[None, :]

    def per_head(pieces):
        query_head, key_head, value_head = pieces
        scores = jnp.dot(query_head, key_head.T, precision=lax.Precision.HIGHEST, preferred_element_type=jnp.float32) * HD ** (-0.5)
        scores = low_back(jnp.where(same_image, scores, -1e+30))
        chances = low(jax.nn.softmax(scores, axis=-1))
        return jnp.dot(chances, value_head, precision=lax.Precision.HIGHEST, preferred_element_type=jnp.float32)
    mixture = lax.map(jax.checkpoint(per_head), (to_heads(queries), to_heads(key_rows), to_heads(value_rows)))
    return mixture.transpose(1, 0, 2).reshape(queries.shape[0], D)

def block_row(tokens, condition, image_row, ada_weight, attn_weight, out_weight, up_weight, down_weight, biases):
    ada_offset = biases[:6 * D]
    query_offset = biases[6 * D:7 * D]
    value_offset = biases[7 * D:8 * D]
    out_offset = biases[8 * D:9 * D]
    up_offset = biases[9 * D:9 * D + FF]
    down_offset = biases[9 * D + FF:]
    cond_act = low(jax.nn.silu(condition))
    modulation = low_back(dense(cond_act, ada_weight, ada_offset))
    shift_mix, scale_mix, gate_mix, shift_feed, scale_feed, gate_feed = jnp.split(modulation, 6, axis=-1)
    attn_input = low(modulate(tokens, shift_mix, scale_mix))
    qkv_offset = jnp.concatenate([query_offset, jnp.zeros_like(query_offset), value_offset])
    projected = low_back(low(dense(attn_input, attn_weight, qkv_offset)))
    attn_out = low_back(low(attend(projected[:, :D], projected[:, D:2 * D], projected[:, 2 * D:], image_row)))
    branch_mix = low_back(dense(attn_out, out_weight, out_offset))
    middle = tokens + gate_mix * branch_mix
    feed_input = low(modulate(middle, shift_feed, scale_feed))
    hidden = low_back(dense(feed_input, up_weight, up_offset))
    active = low(jax.nn.gelu(hidden, approximate=True))
    branch_feed = low_back(dense(active, down_weight, down_offset))
    return middle + gate_feed * branch_feed

def widen(values):
    return values.astype(jnp.float32)

def reference(tokens, condition, image_ids, ada_weight, attn_weight, out_weight, up_weight, down_weight, biases, cotangent):
    params = (widen(ada_weight), widen(attn_weight), widen(out_weight), widen(up_weight), widen(down_weight), widen(biases))

    def per_row(totals, row):
        token_row, cond_row, image_row, grad_row = row

        def forward(token_in, cond_in, *weights):
            return block_row(token_in, cond_in, image_row, *weights)
        result, pull = jax.vjp(forward, widen(token_row), widen(cond_row), *params)
        gradients = pull(widen(grad_row))
        updated = tuple((total + extra for total, extra in zip(totals, gradients[2:])))
        return (updated, (result.astype(jnp.bfloat16), gradients[0], gradients[1]))
    start = tuple((jnp.zeros_like(param) for param in params))
    totals, outputs = lax.scan(per_row, start, (tokens, condition, image_ids, cotangent))
    return (outputs[0], outputs[1], outputs[2], totals[0], totals[1], totals[2], totals[3], totals[4], totals[5])
```

```python
import functools
import math
from functools import partial

import jax
import jax.numpy as jnp
from jax import lax
from jax.experimental import pallas as pl
from jax.experimental.pallas import tpu as pltpu
from jax.sharding import PartitionSpec as P

D = 1152
HEADS = 16
HD = 72
FF = 4608
EPS = 1e-06
F32 = jnp.float32
BF = jnp.bfloat16
ROOT = HD ** (-0.5)
C2 = ROOT * math.log2(math.e)
BIG = 1e30
IMAGES = 9
NN = (((1,), (0,)), ((), ()))
NT = (((1,), (1,)), ((), ()))
TN = (((0,), (0,)), ((), ()))


def dot(a, b, dims=NN):
    return lax.dot_general(a, b, dims, preferred_element_type=F32)


def lanes(n, w):
    return lax.broadcasted_iota(jnp.int32, (n, w), 1)


def pick(width, out_width, offset, copies):
    r = lax.broadcasted_iota(jnp.int32, (width, out_width), 0) - offset
    c = lax.broadcasted_iota(jnp.int32, (width, out_width), 1)
    hit = (r == c) & (c < HD)
    if copies == 2:
        hit = hit | ((r == c - HD) & (c >= HD) & (c < 2 * HD))
    return jnp.where(hit, 1.0, 0.0).astype(BF)


def split3(v):
    a = v.astype(BF).astype(F32)
    r = v - a
    b = r.astype(BF).astype(F32)
    return a, b, r - b


def aug_query(q_block, h, ids, extra=None):
    n, w = q_block.shape
    q = dot(q_block, pick(w, 256, h * HD, 2)) * C2
    lane = lanes(n, 256)
    hi = q.astype(BF).astype(F32)
    out = jnp.where(lane < HD, hi, q - hi)
    out = jnp.where(lane == 2 * HD + ids, BIG, out)
    if extra is not None:
        for t, part in enumerate(split3(extra)):
            out = jnp.where(lane == 2 * HD + IMAGES + t, part, out)
    return out.astype(BF)


def aug_key(k_block, h, ids):
    n, w = k_block.shape
    k = dot(k_block, pick(w, 256, h * HD, 2))
    lane = lanes(n, 256)
    tag = (lane >= 2 * HD) & (lane < 2 * HD + IMAGES) & (lane != 2 * HD + ids)
    out = jnp.where(tag, -1.0, k)
    out = jnp.where((lane >= 2 * HD + IMAGES) & (lane < 2 * HD + IMAGES + 3), 1.0, out)
    return out.astype(BF)


def aug_value(v_block, h, ones):
    n, w = v_block.shape
    v = dot(v_block, pick(w, 128, h * HD, 1))
    lane = lanes(n, 128)
    return jnp.where((lane >= HD) & (lane < HD + ones), 1.0, v).astype(BF)


def forward_kernel(
    hpd, tq, tk, lo_ref, hi_ref, qkv_q, qkv_ref, ids_q, ids_ref, o_ref, lse_ref,
    kaug, vaug, s_scr, qa_scr, best_scr, acc_scr,
):
    r = pl.program_id(0)
    i = pl.program_id(1)
    w = hpd * HD
    length = qkv_ref.shape[1]

    @pl.when(i == 0)
    def _():
        def build(j, _):
            rows = pl.ds(pl.multiple_of(j * tk, tk), tk)
            ids = ids_ref[0, rows, :]
            kb = qkv_ref[0, rows, w : 2 * w]
            vb = qkv_ref[0, rows, 2 * w : 3 * w]
            for h in range(hpd):
                kaug[h, rows, :] = aug_key(kb, h, ids)
                vaug[h, rows, :] = aug_value(vb, h, 1)
            return 0

        lax.fori_loop(0, length // tk, build, 0)

    lo = lo_ref[r, i]
    hi = hi_ref[r, i]
    qb = qkv_q[0, :, 0:w]
    ids = ids_q[0]
    lane = lanes(tq, 128)
    for h in range(hpd):
        qa_scr[h] = aug_query(qb, h, ids)
    best_scr[...] = jnp.full((hpd, tq, 128), -3e38, F32)
    acc_scr[...] = jnp.zeros((hpd, tq, 128), F32)

    def first(j, _):
        rows = pl.ds(pl.multiple_of(j * tk, tk), tk)
        for h in range(hpd):
            s = dot(qa_scr[h], kaug[h, rows, :], NT)
            s_scr[h, :, rows] = s
            best = s[:, 0:128]
            for t in range(1, tk // 128):
                best = jnp.maximum(best, s[:, t * 128 : (t + 1) * 128])
            best_scr[h] = jnp.maximum(best_scr[h], best)
        return 0

    lax.fori_loop(lo, hi, first, 0)
    for h in range(hpd):
        best_scr[h] = jnp.broadcast_to(jnp.max(best_scr[h], axis=1, keepdims=True), (tq, 128))

    def second(j, _):
        rows = pl.ds(pl.multiple_of(j * tk, tk), tk)
        for h in range(hpd):
            top = best_scr[h]
            s = s_scr[h, :, rows]
            p = jnp.concatenate(
                [
                    jnp.exp2(s[:, t * 128 : (t + 1) * 128] - top).astype(BF)
                    for t in range(tk // 128)
                ],
                axis=1,
            )
            acc_scr[h] += dot(p, vaug[h, rows, :])
        return 0

    lax.fori_loop(lo, hi, second, 0)
    out = jnp.zeros((tq, w), F32)
    lse_all = jnp.zeros((tq, 128), F32)
    for h in range(hpd):
        acc = acc_scr[h]
        total = acc[:, HD : HD + 1]
        o = (acc / total).astype(BF)
        o = jnp.where(lane < HD, o, 0).astype(BF)
        out = out + dot(o, pick(w, 128, h * HD, 1), NT)
        lse_all = jnp.where(lane == h, best_scr[h] + jnp.log2(total), lse_all)
    o_ref[0] = out.astype(BF)
    lse_ref[0] = lse_all


def attend_forward(qkv, ids, hpd, tq, tk):
    rows, length, _ = qkv.shape
    w = hpd * HD
    lo, hi = block_ranges(ids, tq, tk)
    column = ids[..., None]
    return pl.pallas_call(
        partial(forward_kernel, hpd, tq, tk),
        grid_spec=pltpu.PrefetchScalarGridSpec(
            num_scalar_prefetch=2,
            grid=(rows, length // tq),
            in_specs=[
                pl.BlockSpec((1, tq, 3 * w), lambda r, i, *_: (r, i, 0)),
                pl.BlockSpec((1, length, 3 * w), lambda r, i, *_: (r, 0, 0)),
                pl.BlockSpec((1, tq, 1), lambda r, i, *_: (r, i, 0)),
                pl.BlockSpec((1, length, 1), lambda r, i, *_: (r, 0, 0)),
            ],
            out_specs=[
                pl.BlockSpec((1, tq, w), lambda r, i, *_: (r, i, 0)),
                pl.BlockSpec((1, tq, 128), lambda r, i, *_: (r, i, 0)),
            ],
            scratch_shapes=[
                pltpu.VMEM((hpd, length, 256), BF),
                pltpu.VMEM((hpd, length, 128), BF),
                pltpu.VMEM((hpd, tq, length), F32),
                pltpu.VMEM((hpd, tq, 256), BF),
                pltpu.VMEM((hpd, tq, 128), F32),
                pltpu.VMEM((hpd, tq, 128), F32),
            ],
        ),
        out_shape=[
            jax.ShapeDtypeStruct((rows, length, w), BF),
            jax.ShapeDtypeStruct((rows, length, 128), F32),
        ],
        compiler_params=pltpu.CompilerParams(vmem_limit_bytes=58 << 20),
        cost_estimate=pl.CostEstimate(
            flops=12 * length * length * rows * w,
            bytes_accessed=8 * rows * length * w,
            transcendentals=rows * length * length * hpd,
        ),
        name="attend_forward",
    )(lo, hi, qkv, qkv, column, column)


def backward_kernel(
    hpd, tq, tk, lo_ref, hi_ref, qkv_ref, g_ref, o_ref, lse_ref, ids_ref, dp_ref,
    qaug, qraw, gaug, dq, kaug, vaug, dka, dva,
):
    r = pl.program_id(0)
    w = hpd * HD
    length = qkv_ref.shape[1]
    step = 256

    def build(i, _):
        rows = pl.ds(pl.multiple_of(i * step, step), step)
        ids = ids_ref[0, rows, :]
        lane = lanes(step, 128)
        qb = qkv_ref[0, rows, 0:w]
        kb = qkv_ref[0, rows, w : 2 * w]
        vb = qkv_ref[0, rows, 2 * w : 3 * w]
        for h in range(hpd):
            lse = lse_ref[0, rows, h : h + 1]
            qaug[h, rows, :] = aug_query(qb, h, ids, -lse)
            e = pick(w, 128, h * HD, 1)
            qraw[h, rows, :] = dot(qb, e).astype(BF)
            g = dot(g_ref[0, rows, :], e)
            o = dot(o_ref[0, rows, :], e)
            delta = jnp.sum(g * o, axis=1, keepdims=True)
            for t, part in enumerate(split3(-delta)):
                g = jnp.where(lane == HD + t, part, g)
            gaug[h, rows, :] = g.astype(BF)
            kaug[h, rows, :] = aug_key(kb, h, ids)
            vaug[h, rows, :] = aug_value(vb, h, 3)
            dq[h, rows, :] = jnp.zeros((step, 128), F32)
        return 0

    lax.fori_loop(0, length // step, build, 0)

    def put(values, n):
        lane = lanes(n, 128)
        full = None
        for h in range(hpd):
            part = dot(
                jnp.where(lane < HD, values[h], 0).astype(BF), pick(w, 128, h * HD, 1), NT
            )
            full = part if full is None else full + part
        return full.astype(BF)

    def per_key(j, _):
        krows = pl.ds(pl.multiple_of(j * tk, tk), tk)
        dka[...] = jnp.zeros((hpd, tk, 128), F32)
        dva[...] = jnp.zeros((hpd, tk, 128), F32)

        def per_query(i, _):
            rows = pl.ds(pl.multiple_of(i * tq, tq), tq)
            for h in range(hpd):
                ka = kaug[h, krows, :]
                va = vaug[h, krows, :]
                ga = gaug[h, rows, :]
                p = jnp.exp2(dot(ka, qaug[h, rows, :], NT))
                dp = dot(va, ga, NT)
                dva[h] += dot(p.astype(BF), ga)
                ds = (p * dp).astype(BF)
                dka[h] += dot(ds, qraw[h, rows, :])
                dq[h, rows, :] += dot(ds, ka[:, :128], TN)
            return 0

        lax.fori_loop(lo_ref[r, j], hi_ref[r, j], per_query, 0)
        dp_ref[0, krows, w : 2 * w] = put([dka[h] * ROOT for h in range(hpd)], tk)
        dp_ref[0, krows, 2 * w : 3 * w] = put([dva[h] for h in range(hpd)], tk)
        return 0

    lax.fori_loop(0, length // tk, per_key, 0)

    def finish(i, _):
        rows = pl.ds(pl.multiple_of(i * step, step), step)
        dp_ref[0, rows, 0:w] = put([dq[h, rows, :] * ROOT for h in range(hpd)], step)
        return 0

    lax.fori_loop(0, length // step, finish, 0)


def attend_backward(qkv, g, o, lse, ids, hpd, tq, tk):
    rows, length, _ = qkv.shape
    w = hpd * HD
    lo, hi = block_ranges(ids, tk, tq)

    def spec(n):
        return pl.BlockSpec((1, length, n), lambda r, *_: (r, 0, 0))

    return pl.pallas_call(
        partial(backward_kernel, hpd, tq, tk),
        grid_spec=pltpu.PrefetchScalarGridSpec(
            num_scalar_prefetch=2,
            grid=(rows,),
            in_specs=[spec(3 * w), spec(w), spec(w), spec(128), spec(1)],
            out_specs=spec(3 * w),
            scratch_shapes=[
                pltpu.VMEM((hpd, length, 256), BF),
                pltpu.VMEM((hpd, length, 128), BF),
                pltpu.VMEM((hpd, length, 128), BF),
                pltpu.VMEM((hpd, length, 128), F32),
                pltpu.VMEM((hpd, length, 256), BF),
                pltpu.VMEM((hpd, length, 128), BF),
                pltpu.VMEM((hpd, tk, 128), F32),
                pltpu.VMEM((hpd, tk, 128), F32),
            ],
        ),
        out_shape=jax.ShapeDtypeStruct((rows, length, 3 * w), BF),
        compiler_params=pltpu.CompilerParams(vmem_limit_bytes=58 << 20),
        cost_estimate=pl.CostEstimate(
            flops=30 * length * length * rows * w,
            bytes_accessed=18 * rows * length * w,
            transcendentals=rows * length * length * hpd,
        ),
        name="attend_backward",
    )(lo, hi, qkv, g, o, lse, ids[..., None])


def block_ranges(ids, mine, theirs):
    rows, length = ids.shape
    own = ids.reshape(rows, length // mine, mine)
    far = ids.reshape(rows, length // theirs, theirs)
    before = far[:, None, :, -1] < own[:, :, None, 0]
    reached = far[:, None, :, 0] <= own[:, :, None, -1]
    return (
        jnp.sum(before.astype(jnp.int32), axis=-1),
        jnp.sum(reached.astype(jnp.int32), axis=-1),
    )


def params(mib=58):
    return pltpu.CompilerParams(vmem_limit_bytes=mib << 20)


def cost(units, count, moved):
    return pl.CostEstimate(
        flops=int(2 * units * count * D * D), bytes_accessed=int(moved), transcendentals=0
    )


def once(shape, index):
    return pl.BlockSpec(shape, index, pipeline_mode=pl.Buffered(1))


def row_tile(count):
    return 288 if count % 288 == 0 else count


def norm_of(values):
    center = values - jnp.mean(values, axis=-1, keepdims=True)
    spread = jnp.mean(center * center, axis=-1, keepdims=True)
    inverse = lax.rsqrt(spread + EPS)
    return center * inverse, inverse


def norm_back(gradient, n, inverse):
    return (
        gradient
        - jnp.mean(gradient, axis=-1, keepdims=True)
        - n * jnp.mean(gradient * n, axis=-1, keepdims=True)
    ) * inverse


def mix_input_kernel(cond_ref, x_ref, ada_ref, bias_ref, act_ref, input_ref, scale_ref):
    cond = cond_ref[...].astype(F32)
    act = (cond / (1.0 + jnp.exp(-cond))).astype(BF)
    act_ref[...] = act
    parts = [dot(act, ada_ref[i]) for i in range(4)]
    shift = jnp.concatenate(parts[:2], axis=1) + bias_ref[0]
    scale = jnp.concatenate(parts[2:], axis=1) + bias_ref[1]
    normed, _ = norm_of(x_ref[...].astype(F32))
    scale_ref[...] = scale.astype(BF)
    input_ref[...] = (normed * (1.0 + scale) + shift).astype(BF)


def mix_input(cond, x, ada, bias):
    count = cond.shape[0]
    tm = row_tile(count)
    rows = pl.BlockSpec((tm, D), lambda i: (i, 0))
    return pl.pallas_call(
        mix_input_kernel,
        grid=(count // tm,),
        in_specs=[rows, rows, once((4, D, D // 2), lambda i: (0, 0, 0)),
                  once((2, 1, D), lambda i: (0, 0, 0))],
        out_specs=[rows, rows, rows],
        out_shape=[jax.ShapeDtypeStruct((count, D), BF)] * 3,
        compiler_params=params(),
        cost_estimate=cost(2, count, 10 * count * D + 4 * D * D),
        name="mix_input",
    )(cond, x, ada, bias)


def before_feed_kernel(
    act_ref, attn_ref, x_ref, cot_ref, ada_ref, out_ref, ada_bias, out_bias,
    gates_ref, mix_ref, middle_ref, input_ref, grad_ref,
):
    act = act_ref[...]
    gate_mix = dot(act, ada_ref[0]) + ada_bias[0]
    gates_ref[0] = gate_mix.astype(BF)
    branch_mix = dot(attn_ref[...], out_ref[...]) + out_bias[...]
    mix_ref[...] = branch_mix.astype(BF)
    middle = x_ref[...].astype(F32) + gate_mix * branch_mix
    middle_ref[...] = middle
    normed, _ = norm_of(middle)
    scale_feed = dot(act, ada_ref[2]) + ada_bias[2]
    gates_ref[1] = scale_feed.astype(BF)
    shift_feed = dot(act, ada_ref[1]) + ada_bias[1]
    input_ref[...] = (normed * (1.0 + scale_feed) + shift_feed).astype(BF)
    gate_feed = dot(act, ada_ref[3]) + ada_bias[3]
    gates_ref[2] = gate_feed.astype(BF)
    grad_ref[...] = (cot_ref[...].astype(F32) * gate_feed).astype(BF)


def before_feed(act, attn_out, x, cot, ada, out_mat, ada_bias, out_bias):
    count = act.shape[0]
    tm = row_tile(count)
    rows = pl.BlockSpec((tm, D), lambda i: (i, 0))
    return pl.pallas_call(
        before_feed_kernel,
        grid=(count // tm,),
        in_specs=[rows, rows, rows, rows, once((4, D, D), lambda i: (0, 0, 0)),
                  once((D, D), lambda i: (0, 0)), once((4, 1, D), lambda i: (0, 0, 0)),
                  once((1, D), lambda i: (0, 0))],
        out_specs=[pl.BlockSpec((3, tm, D), lambda i: (0, i, 0)), rows, rows, rows, rows],
        out_shape=[
            jax.ShapeDtypeStruct((3, count, D), BF),
            jax.ShapeDtypeStruct((count, D), BF),
            jax.ShapeDtypeStruct((count, D), F32),
            jax.ShapeDtypeStruct((count, D), BF),
            jax.ShapeDtypeStruct((count, D), BF),
        ],
        compiler_params=params(),
        cost_estimate=cost(5, count, 24 * count * D + 10 * D * D),
        name="before_feed",
    )(act, attn_out, x, cot, ada, out_mat, ada_bias, out_bias)


GELU_A = math.sqrt(2.0 / math.pi)
GELU_B = 0.044715


def feed_kernel(
    tm, input_ref, grad_ref, up_ref, down_ref, bias_ref,
    branch_out, shift_out, up_grad_ref, down_grad_ref, bias_grad_ref,
    branch, shift, active, hidden_grad, sem,
):
    t = pl.program_id(0)
    count = input_ref.shape[0]

    @pl.when(t == 0)
    def _():
        branch[...] = jnp.zeros_like(branch)
        shift[...] = jnp.zeros_like(shift)

    total = jnp.zeros((1, active.shape[1]), F32)
    for m in range(count // tm):
        rows = slice(m * tm, (m + 1) * tm)
        h = dot(input_ref[rows, :], up_ref[0]) + bias_ref[0]
        square = h * h
        th = jnp.tanh(GELU_A * h * (1.0 + GELU_B * square))
        half = 0.5 * (1.0 + th)
        act = (h * half).astype(BF)
        slope = half + (0.5 * GELU_A) * h * (1.0 - th * th) * (1.0 + 3.0 * GELU_B * square)
        active[rows, :] = act
        hidden = dot(grad_ref[rows, :], down_ref[0], NT) * slope
        low = hidden.astype(BF)
        hidden_grad[rows, :] = low
        total = total + jnp.sum(low.astype(F32), axis=0, keepdims=True)
        branch[rows, :] += dot(act, down_ref[0])
        shift[rows, :] += dot(low, up_ref[0], NT)
    bias_grad_ref[0] = total
    down_grad_ref[0] = dot(active[...], grad_ref[...], TN).astype(BF)
    up_grad_ref[0] = dot(input_ref[...], hidden_grad[...], TN).astype(BF)

    @pl.when(t == pl.num_programs(0) - 1)
    def _():
        first = pltpu.make_async_copy(branch, branch_out, sem.at[0])
        second = pltpu.make_async_copy(shift, shift_out, sem.at[1])
        first.start()
        second.start()
        first.wait()
        second.wait()


def feed(feed_input, feed_grad, ups, downs, up_bias):
    count = feed_input.shape[0]
    seqs, _, nf = ups.shape
    tm = 384 if count % 384 == 0 else count
    whole = once((count, D), lambda t: (0, 0))
    place = lambda t: (t, 0, 0)
    return pl.pallas_call(
        partial(feed_kernel, tm),
        grid_spec=pltpu.PrefetchScalarGridSpec(
            num_scalar_prefetch=0,
            grid=(seqs,),
            in_specs=[whole, whole, pl.BlockSpec((1, D, nf), place), pl.BlockSpec((1, nf, D), place),
                      pl.BlockSpec((1, 1, nf), place)],
            out_specs=[
                pl.BlockSpec(memory_space=pl.ANY),
                pl.BlockSpec(memory_space=pl.ANY),
                pl.BlockSpec((1, D, nf), place),
                pl.BlockSpec((1, nf, D), place),
                pl.BlockSpec((1, 1, nf), place),
            ],
            scratch_shapes=[
                pltpu.VMEM((count, D), F32),
                pltpu.VMEM((count, D), F32),
                pltpu.VMEM((count, nf), BF),
                pltpu.VMEM((count, nf), BF),
                pltpu.SemaphoreType.DMA((2,)),
            ],
        ),
        out_shape=[
            jax.ShapeDtypeStruct((count, D), F32),
            jax.ShapeDtypeStruct((count, D), F32),
            jax.ShapeDtypeStruct((seqs, D, nf), BF),
            jax.ShapeDtypeStruct((seqs, nf, D), BF),
            jax.ShapeDtypeStruct((seqs, 1, nf), F32),
        ],
        compiler_params=params(62),
        cost_estimate=cost(24 * FF // (4 * D), count, 16 * count * D + 8 * FF * D),
        name="feed",
    )(feed_input, feed_grad, ups, downs, up_bias)


def after_feed_kernel(
    branch_ref, shift_ref, middle_ref, gates_ref, mix_ref, cot_ref, out_ref, bias_ref,
    block_ref, late_ref, mix_grad_ref, attn_grad_ref, middle_grad_ref,
):
    cot = cot_ref[...].astype(F32)
    middle = middle_ref[...]
    branch = branch_ref[...] + bias_ref[...]
    block_ref[...] = (middle + gates_ref[2].astype(F32) * branch).astype(BF)
    late_ref[3] = (cot * branch).astype(BF)
    shift = shift_ref[...]
    late_ref[1] = shift.astype(BF)
    normed, inverse = norm_of(middle)
    late_ref[2] = (shift * normed).astype(BF)
    middle_grad = cot + norm_back(shift * (1.0 + gates_ref[1].astype(F32)), normed, inverse)
    middle_grad_ref[...] = middle_grad
    late_ref[0] = (middle_grad * mix_ref[...].astype(F32)).astype(BF)
    mix_grad = (middle_grad * gates_ref[0].astype(F32)).astype(BF)
    mix_grad_ref[...] = mix_grad
    attn_grad_ref[...] = dot(mix_grad, out_ref[...], NT).astype(BF)


def after_feed(branch, shift, middle, gates, mix, cot, out_mat, down_bias):
    count = branch.shape[0]
    tm = row_tile(count)
    rows = pl.BlockSpec((tm, D), lambda i: (i, 0))
    return pl.pallas_call(
        after_feed_kernel,
        grid=(count // tm,),
        in_specs=[rows, rows, rows, pl.BlockSpec((3, tm, D), lambda i: (0, i, 0)), rows, rows,
                  once((D, D), lambda i: (0, 0)), once((1, D), lambda i: (0, 0))],
        out_specs=[rows, pl.BlockSpec((4, tm, D), lambda i: (0, i, 0)), rows, rows, rows],
        out_shape=[
            jax.ShapeDtypeStruct((count, D), BF),
            jax.ShapeDtypeStruct((4, count, D), BF),
            jax.ShapeDtypeStruct((count, D), BF),
            jax.ShapeDtypeStruct((count, D), BF),
            jax.ShapeDtypeStruct((count, D), F32),
        ],
        compiler_params=params(),
        cost_estimate=cost(1, count, 44 * count * D),
        name="after_feed",
    )(branch, shift, middle, gates, mix, cot, out_mat, down_bias)


def token_products_kernel(order, act_ref, grad_ref, out_ref, sum_ref):
    grad = grad_ref[0]
    out_ref[0] = dot(act_ref[...], grad, TN).astype(BF)
    sum_ref[0] = jnp.sum(grad.astype(F32), axis=0, keepdims=True)


def token_products(order, act, grads):
    parts, count, _ = grads.shape
    return pl.pallas_call(
        token_products_kernel,
        grid_spec=pltpu.PrefetchScalarGridSpec(
            num_scalar_prefetch=1,
            grid=(parts,),
            in_specs=[once((count, D), lambda t, o: (0, 0)),
                      pl.BlockSpec((1, count, D), lambda t, o: (o[t], 0, 0))],
            out_specs=[pl.BlockSpec((1, D, D), lambda t, o: (t, 0, 0)),
                       pl.BlockSpec((1, 1, D), lambda t, o: (o[t], 0, 0))],
        ),
        out_shape=[
            jax.ShapeDtypeStruct((parts, D, D), BF),
            jax.ShapeDtypeStruct((parts, 1, D), F32),
        ],
        compiler_params=params(),
        cost_estimate=cost(parts, count, 2 * (parts + 1) * count * D + 2 * parts * D * D),
        name="token_products",
    )(order, act, grads)


def to_condition_kernel(parts, last, grads_ref, ada_ref, *refs):
    out_ref, total = refs[-2:]
    t = pl.program_id(1)
    part = dot(grads_ref[0], ada_ref[0], NT)

    @pl.when(t == 0)
    def _():
        total[...] = part + refs[0][...] if last else part

    @pl.when(t > 0)
    def _():
        total[...] += part

    @pl.when(t == parts - 1)
    def _():
        if last:
            cond = refs[1][...].astype(F32)
            gate = 1.0 / (1.0 + jnp.exp(-cond))
            out_ref[...] = total[...] * (gate * (1.0 + cond * (1.0 - gate)))
        else:
            out_ref[...] = total[...]


def to_condition(grads, ada, *rest):
    parts, count, _ = grads.shape
    tm = count // 2 if count % 32 == 0 else count
    rows = pl.BlockSpec((tm, D), lambda m, t: (m, 0))
    return pl.pallas_call(
        partial(to_condition_kernel, parts, len(rest) > 0),
        grid=(count // tm, parts),
        in_specs=[pl.BlockSpec((1, tm, D), lambda m, t: (t, m, 0)),
                  pl.BlockSpec((1, D, D), lambda m, t: (t, 0, 0))] + [rows] * len(rest),
        out_specs=rows,
        scratch_shapes=[pltpu.VMEM((tm, D), F32)],
        out_shape=jax.ShapeDtypeStruct((count, D), F32),
        compiler_params=params(),
        cost_estimate=cost(parts, count, 2 * parts * count * D + 12 * count * D),
        name="to_condition",
    )(grads, ada, *rest)


class Places:
    def __init__(self, packs, seqs):
        self.packs, self.seqs = packs, seqs
        self.rings, self.sides = packs // 2, seqs // 2
        self.pack = lax.axis_index("pack")
        self.seq = lax.axis_index("seq")
        self.a, self.b = self.pack // 2, self.pack % 2
        self.y, self.c = self.seq // 2, self.seq % 2

    def ring(self, value, k):
        n = self.rings
        pairs = [(a * 2 + b, ((a + k) % n) * 2 + b) for a in range(n) for b in range(2)]
        return lax.ppermute(value, "pack", pairs)

    def cross(self, value):
        return lax.ppermute(value, "pack", [(p, p ^ 1) for p in range(self.packs)])

    def side(self, value, k):
        n = self.sides
        pairs = [(y * 2 + c, ((y + k) % n) * 2 + c) for y in range(n) for c in range(2)]
        return lax.ppermute(value, "seq", pairs)

    def core(self, value):
        return lax.ppermute(value, "seq", [(s, s ^ 1) for s in range(self.seqs)])

    def gather_by(self, shard, members):
        groups = [[p * self.seqs + s for s in group for p in range(self.packs)] for group in members]
        out = lax.all_gather(
            shard, ("pack", "seq"), axis=0, tiled=True, axis_index_groups=groups
        )
        return out.reshape((len(members[0]), self.packs) + shard.shape)

    def gather_seq(self, value):
        whole = jnp.zeros((self.seqs,) + value.shape, value.dtype)
        rest = (0,) * value.ndim
        for k in range(self.sides):
            block = value if k == 0 else self.side(value, k)
            side = (self.y - k + self.sides) % self.sides
            whole = lax.dynamic_update_slice(whole, block[None], (side * 2 + self.c,) + rest)
            whole = lax.dynamic_update_slice(
                whole, self.core(block)[None], (side * 2 + 1 - self.c,) + rest
            )
        return whole

    def two(self, own, other):
        return jnp.where(self.c == 0, own, other), jnp.where(self.c == 0, other, own)

    def ring_blocks(self, value):
        return [value if k == 0 else self.ring(value, k) for k in range(self.rings)]

    def ring_join(self, blocks):
        rest = (0,) * blocks[0].ndim
        part = jnp.zeros((self.rings,) + blocks[0].shape, blocks[0].dtype)
        for k, block in enumerate(blocks):
            place = (self.a - k + self.rings) % self.rings
            part = lax.dynamic_update_slice(part, block[None], (place,) + rest)
        return part

    def cross_join(self, part, other):
        rest = (0,) * (part.ndim - 1)
        whole = jnp.zeros((self.rings, 2) + part.shape[1:], part.dtype)
        whole = lax.dynamic_update_slice(whole, part[:, None], (0, self.b) + rest)
        whole = lax.dynamic_update_slice(whole, other[:, None], (0, 1 - self.b) + rest)
        return whole.reshape((self.packs,) + part.shape[1:])

    def gather_pack(self, value):
        part = self.ring_join(self.ring_blocks(value))
        return self.cross_join(part, self.cross(part))

    def scatter_all(self, whole):
        r, n = whole.shape[2:]
        order = [[p * self.seqs + s for s in range(self.seqs) for p in range(self.packs)]]
        return lax.psum_scatter(
            whole.reshape(-1, n), ("pack", "seq"), scatter_dimension=0, tiled=True,
            axis_index_groups=order,
        )

    def reduce_core(self, pieces):
        give = lax.dynamic_index_in_dim(pieces, 1 - self.c, 1, False)
        keep = lax.dynamic_index_in_dim(pieces, self.c, 1, False)
        return add(keep, self.core(give), kind=pieces.dtype)

    def reduce_cross(self, whole):
        split = whole.reshape((whole.shape[0], self.rings, 2) + whole.shape[2:])
        give = lax.dynamic_index_in_dim(split, 1 - self.b, 2, False)
        keep = lax.dynamic_index_in_dim(split, self.b, 2, False)
        return add(keep, self.cross(give), kind=whole.dtype)

    def reduce_ring(self, part):
        groups = [[a * 2 + b for a in range(self.rings)] for b in range(2)]
        parts = lax.all_to_all(part, "pack", 1, 1, axis_index_groups=groups, tiled=True)
        return jnp.sum(parts.astype(F32), axis=1)

    def reduce_pack(self, whole):
        return self.reduce_ring(self.reduce_cross(whole[None]))[0]

    def reduce_side(self, pieces):
        terms = [lax.dynamic_index_in_dim(pieces, self.y, 0, False)]
        for k in range(1, self.sides):
            block = lax.dynamic_index_in_dim(pieces, (self.y + k) % self.sides, 0, False)
            terms.append(self.side(block, k))
        return add(*terms, kind=pieces.dtype)

def after(value, first):
    return lax.optimization_barrier((value, first))


def add(*terms, kind=BF):
    total = terms[0].astype(F32)
    for term in terms[1:]:
        total = total + term.astype(F32)
    return total.astype(kind)


def token_sum(gradient):
    return jnp.sum(gradient.astype(F32), axis=0)


def per_device(packs, seqs, tokens, condition, image_ids, ada_weight, attn_weight, out_weight,
               up_weight, down_weight, biases, cotangent):
    at = Places(packs, seqs)
    rows, own = image_ids.shape
    length = own * seqs
    count = rows * own
    hpd = HEADS // seqs
    w = hpd * HD
    r = D // packs
    rf = FF // packs
    n2 = 4 * D // seqs
    nf = FF // seqs

    bias_len = biases.shape[0]
    padded = -(-bias_len // 512) * 512
    half = D // 2
    ids = at.gather_seq(image_ids).transpose(1, 0, 2).reshape(rows, length)
    first = jnp.where(ids[0, length - 1] == 0, 0, 1)
    row_order = [first, 1 - first]

    def in_order(values):
        return jnp.where(
            first == 0, jnp.concatenate(values, axis=0), jnp.concatenate(values[::-1], axis=0)
        )

    if seqs == 4:
        left, right = ada_weight[:, :D], ada_weight[:, D:]
        head, tail = ada_weight[:, :half], ada_weight[:, half:]
        side_got = lax.ppermute(jnp.where(at.seq == 0, right, head), "seq", [(0, 2), (1, 3)])
        core_got = lax.ppermute(
            jnp.where(at.seq == 0, jnp.roll(left, half, axis=1), jnp.where(at.seq == 1, tail, left)),
            "seq", [(0, 1), (1, 0), (3, 2)],
        )
        shard1 = jnp.where(at.seq == 0, head, jnp.where(at.seq == 1, core_got[:, :half], side_got))
        shard1, biases, attn_weight, out_weight, down_weight, ada_weight = lax.optimization_barrier(
            (shard1, biases, attn_weight, out_weight, down_weight, ada_weight)
        )
        far_got = lax.ppermute(ada_weight[:, :D], "seq", [(2, 1)])
        merged = jnp.concatenate([ada_weight[:, D:], core_got[:, :half]], axis=1)
        shard2 = jnp.where(
            at.seq == 0, core_got,
            jnp.where(at.seq == 1, far_got, jnp.where(at.seq == 2, merged, ada_weight[:, half:])),
        )
        both = at.gather_seq(jnp.concatenate([attn_weight, out_weight], axis=1))
    else:
        both = lax.all_gather(
            jnp.concatenate([attn_weight, out_weight, ada_weight], axis=1), "seq", axis=0
        )
        ada_rows = both[:, :, attn_weight.shape[1] + out_weight.shape[1] :]
        ada_rows = ada_rows.transpose(1, 0, 2).reshape(r, 6 * D)
        shard1 = lax.dynamic_slice_in_dim(ada_rows, at.seq * (n2 // 2), n2 // 2, 1)
        shard2 = lax.dynamic_slice_in_dim(ada_rows, 2 * D + at.seq * n2, n2, 1)
    cut = attn_weight.shape[1]
    attn_rows = both[:, :, :cut].transpose(1, 0, 2).reshape(r, 3 * D)
    out_rows = both[:, :, cut : cut + out_weight.shape[1]].transpose(1, 0, 2).reshape(r, D)
    every = [range(seqs)]
    ada1 = at.gather_by(shard1, every)
    ada1 = ada1.reshape(4, seqs // 4, D, n2 // 2).transpose(0, 2, 1, 3).reshape(4, D, half)
    mine = lax.dynamic_slice_in_dim(attn_rows.reshape(r, 3, seqs, w), at.seq, 1, 2)
    attn_blocks = at.ring_blocks(mine.reshape(r, 3 * w))
    lined = jnp.pad(biases, (0, padded - bias_len)).reshape(-1, 128)
    offsets = at.gather_pack(at.gather_seq(lined)).reshape(packs, seqs, padded)
    offsets = offsets[:, :, :bias_len].reshape(-1)

    ada2 = at.gather_by(shard2, every)
    ada2 = ada2.reshape(4, seqs // 4, D, n2).transpose(0, 2, 1, 3).reshape(4, D, D)
    rq = rf // seqs
    down_rows = lax.all_to_all(down_weight, "seq", 0, 1, tiled=True)
    down_rows, up_weight, ada1 = lax.optimization_barrier((down_rows, up_weight, ada1))
    down_mat = lax.all_gather(down_rows, ("pack", "seq"), axis=0, tiled=True)
    down_mats = down_mat.reshape(seqs, nf, D)
    up_mats = at.gather_by(up_weight, every).reshape(seqs, D, nf)

    query_offset = offsets[6 * D : 7 * D]
    value_offset = offsets[7 * D : 8 * D]
    out_offset = offsets[8 * D : 9 * D]
    up_offset = offsets[9 * D : 9 * D + FF]
    down_offset = offsets[9 * D + FF :]

    x = tokens.reshape(count, D).astype(F32)
    cond_act, attn_input, scale_mix = mix_input(
        condition.reshape(count, D), tokens.reshape(count, D), ada1,
        offsets[: 2 * D].astype(F32).reshape(2, 1, D),
    )
    attn_input = attn_input.reshape(rows, own, D)
    head_offset = jnp.concatenate(
        [
            lax.dynamic_slice_in_dim(query_offset, at.seq * w, w),
            jnp.zeros((w,), BF),
            lax.dynamic_slice_in_dim(value_offset, at.seq * w, w),
        ]
    )

    wide = 640
    out_half = jnp.where(at.c == 0, out_rows[:, :wide], out_rows[:, D - wide :])
    attn_input, attn_blocks, out_half = lax.optimization_barrier((attn_input, attn_blocks, out_half))
    starts = [lax.dynamic_index_in_dim(attn_input, row, 0, False) for row in row_order]
    attn_part = at.ring_join(attn_blocks)
    attn_mat = at.cross_join(attn_part, at.cross(attn_part)).reshape(D, 3 * w)
    out_blocks = at.ring_blocks(out_half)

    inputs, qkvs, heads, lses, outs = [], [], [], [], []
    id_rows = [lax.dynamic_slice_in_dim(ids, row, 1, 0) for row in row_order]
    for row in range(rows):
        start = starts[row]
        blocks = []
        for k in range(at.sides):
            block = start if k == 0 else at.side(start, k)
            if k and row + 1 < rows:
                starts[row + 1], block = after(starts[row + 1], block)
            if k and row:
                block, heads[row - 1] = after(block, heads[row - 1])
            side = (at.y - k + at.sides) % at.sides
            blocks += [(side * 2 + at.c, block), (side * 2 + 1 - at.c, at.core(block))]
        inputs.append(blocks)
        qkv = jnp.zeros((seqs, own, 3 * w), BF)
        for place, block in blocks:
            part = (dot(block, attn_mat) + head_offset).astype(BF)
            qkv = lax.dynamic_update_slice(qkv, part[None], (place, 0, 0))
        qkvs.append(qkv.reshape(1, length, 3 * w))
        if row == 0:
            qkvs[0], out_blocks = after(qkvs[0], out_blocks)
            out_part = at.ring_join(out_blocks)
            out_other = at.cross(out_part)
        if row == 1:
            qkvs[1], out_other = after(qkvs[1], out_other)
            out_own = at.cross_join(out_part, out_other).reshape(D, wide)
            out_far = at.core(out_own)
        head, lse = attend_forward(qkvs[row], id_rows[row], hpd, 256, 768)
        heads.append(head)
        lses.append(lse)
    for row in range(rows):
        outs.append(lax.all_to_all(heads[row][0], "seq", 0, 1, tiled=True))
    out_left, out_right = at.two(out_own, out_far)
    out_mat = jnp.concatenate([out_left, out_right[:, 2 * wide - D :]], axis=1)

    def line(values, parts):
        return values.astype(F32).reshape(parts + (1, -1))

    attn_out = in_order(outs)
    gates, branch_mix, middle, feed_input, feed_out_grad = before_feed(
        cond_act, attn_out, tokens.reshape(count, D), cotangent.reshape(count, D), ada2, out_mat,
        line(offsets[2 * D : 6 * D], (4,)), line(out_offset, ()),
    )
    branch_feed, shift_sum, up_whole, down_whole, up_sums = feed(
        feed_input, feed_out_grad, up_mats, down_mats, line(up_offset, (seqs,))
    )
    block_out, late, mix_out_grad, attn_out_grad, middle_grad = after_feed(
        branch_feed, shift_sum, middle, gates, branch_mix, cotangent.reshape(count, D), out_mat,
        line(down_offset, ()),
    )

    attn_out_grad = attn_out_grad.reshape(rows, own, D)
    down_part = lax.psum_scatter(
        down_whole.reshape(FF, D), ("pack", "seq"), scatter_dimension=0, tiled=True
    )
    up_grad = at.scatter_all(up_whole.reshape(seqs, packs, r, nf)).astype(F32)
    grad_heads = [
        lax.all_to_all(
            lax.dynamic_index_in_dim(attn_out_grad, row, 0, False), "seq", 1, 0, tiled=True
        )
        for row in row_order
    ]
    out_whole = dot(attn_out, mix_out_grad, TN).astype(BF).reshape(packs, 2, r // 2, D)
    if seqs == 4:
        turn = jnp.stack([y * 2 + core for core in (1 - at.c, at.c) for y in range(2)])
        late_whole, late_sums = token_products(turn.astype(jnp.int32), cond_act, late)
        late_whole = late_whole.reshape(2, 2, packs, r, D)
        late_core = add(late_whole[1], at.core(late_whole[0]))
        out_core = at.reduce_core(out_whole)
        grad_heads[0], late_core, out_core = lax.optimization_barrier(
            (grad_heads[0], late_core, out_core)
        )
        late_pair = at.reduce_cross(late_core)
    else:
        late_whole, late_sums = token_products(jnp.arange(4, dtype=jnp.int32), cond_act, late)
        late_whole = late_whole.reshape(4, packs, r, seqs // 4, n2).transpose(0, 3, 1, 2, 4)
        ada_late = at.scatter_all(late_whole.reshape(seqs, packs, r, n2))
        out_core = at.reduce_core(out_whole)
    out_pair = at.reduce_cross(out_core[None])

    input_grads, flat_grads = [], []
    for row in range(rows):
        if row == 1 and seqs == 4:
            grad_heads[1], late_pair = after(grad_heads[1], late_pair)
            late_ring = at.reduce_ring(late_pair).astype(BF)
        if row == 1:
            grad_heads[1], out_pair = after(grad_heads[1], out_pair)
            out_ring = at.reduce_ring(out_pair)[0].astype(BF)
        grad = attend_backward(
            qkvs[row], grad_heads[row][None], heads[row], lses[row], id_rows[row], hpd, 256, 768
        )[0]
        flat_grads.append(grad)
        part = dot(grad, attn_mat, NT).astype(BF).reshape(at.sides, 2, own, D)
        input_grads.append(at.reduce_side(at.reduce_core(part)))
    late, flat_grads = after(late, flat_grads)
    cond_part = to_condition(late, ada2)
    input_grad = in_order(input_grads)
    out_side = at.reduce_side(out_ring.reshape(r // 2, at.sides, -1).transpose(1, 0, 2))
    out_side = out_side.reshape(r // 2, 2, -1).transpose(1, 0, 2)
    out_far = at.core(lax.dynamic_index_in_dim(out_side, 1 - at.c, 0, False))
    out_near = lax.dynamic_index_in_dim(out_side, at.c, 0, False)
    out_grad = jnp.concatenate(at.two(out_near, out_far)).astype(F32)
    if seqs == 4:
        ada_late = at.reduce_side(late_ring)
    attn_whole = 0.0
    for row in range(rows):
        for place, block in inputs[row]:
            piece = lax.dynamic_slice_in_dim(flat_grads[row], place * own, own, 0)
            attn_whole = attn_whole + dot(block, piece, TN)
    attn_part = at.reduce_pack(attn_whole.astype(BF).reshape(packs, r, 3 * w)).astype(BF)
    norm_x, inverse_x = norm_of(x)
    scale_mix_grad = (input_grad * norm_x).astype(BF)
    tokens_grad = middle_grad + norm_back(input_grad * (1.0 + scale_mix.astype(F32)), norm_x, inverse_x)
    shift_mix_grad = input_grad.astype(BF)
    early = jnp.stack([shift_mix_grad, scale_mix_grad])
    early_whole, early_sums = token_products(
        jnp.stack([1 - at.c, at.c]).astype(jnp.int32), cond_act, early
    )
    early_whole = early_whole.reshape(2, packs, r, D)
    early_core = add(early_whole[1], at.core(early_whole[0]))
    early_pack = at.reduce_pack(early_core).astype(BF)
    early_side = add(early_pack, *[at.side(early_pack, k) for k in range(1, at.sides)])
    ada1_parts = ada1.reshape(2, 2, D, half).transpose(0, 2, 1, 3).reshape(2, D, D)
    condition_grad = to_condition(early, ada1_parts, cond_part, condition.reshape(count, D))

    def own_columns(whole):
        n = whole.shape[1] // seqs
        return lax.dynamic_slice_in_dim(whole, at.seq * n, n, 1).astype(F32)

    if seqs == 4:
        early_half = lax.ppermute(early_side[:, :half], "seq", [(1, 0)])
        swapped = lax.ppermute(ada_late, "seq", [(0, 1), (1, 2)])
        late_half = lax.ppermute(ada_late[:, half:], "seq", [(2, 3)])
        whole_part = jnp.where(
            at.seq == 0, early_side, jnp.where(at.seq == 3, ada_late, swapped)
        )
        half_part = jnp.where(
            at.seq == 1, early_side[:, half:],
            jnp.where(at.seq == 2, ada_late[:, :half], early_half + late_half),
        )
        ada_grad = jnp.where(
            at.c == 0,
            jnp.concatenate([whole_part, half_part], axis=1),
            jnp.concatenate([half_part, whole_part], axis=1),
        ).astype(F32)
    else:
        early_all = jnp.concatenate(at.two(early_side, at.core(early_side)), axis=1)
        late_all = at.gather_seq(ada_late).transpose(1, 0, 2).reshape(r, 4 * D)
        ada_grad = own_columns(jnp.concatenate([early_all, late_all], axis=1))
    attn_all = at.gather_seq(attn_part).reshape(seqs, r, 3, w).transpose(1, 2, 0, 3).reshape(r, 3 * D)

    down_grad = lax.all_to_all(down_part, "seq", 1, 0, tiled=True).astype(F32)

    head_sum = sum(token_sum(g) for g in flat_grads).reshape(3, w)
    zero = jnp.zeros((D,), F32)
    head_sums = [
        lax.dynamic_update_slice_in_dim(zero, head_sum[i], at.seq * w, 0) for i in (0, 2)
    ]
    bias_whole = jnp.concatenate(
        [early_sums.reshape(-1), late_sums.reshape(-1)]
        + head_sums
        + [token_sum(mix_out_grad)]
        + [up_sums.reshape(-1)]
        + [token_sum(feed_out_grad)]
    )
    bias_whole = jnp.pad(bias_whole.reshape(packs, seqs, bias_len), ((0, 0), (0, 0), (0, padded - bias_len)))
    bias_whole = bias_whole.transpose(1, 0, 2).reshape(at.sides, 2, packs, padded // 128, 128)
    bias_part = at.reduce_side(at.reduce_core(bias_whole))
    bias_grad = at.reduce_pack(bias_part).reshape(-1)[:bias_len]
    return (
        block_out.reshape(tokens.shape),
        tokens_grad.reshape(tokens.shape),
        condition_grad.reshape(tokens.shape),
        ada_grad,
        own_columns(attn_all),
        out_grad,
        up_grad,
        down_grad,
        bias_grad,
    )


def solution(mesh):
    acts = P("pack", "seq", None)
    mats = P("pack", "seq")
    vec = P(("pack", "seq"))
    return jax.shard_map(
        partial(per_device, mesh.shape["pack"], mesh.shape["seq"]),
        mesh=mesh,
        in_specs=(acts, acts, mats, mats, mats, mats, mats, mats, vec, acts),
        out_specs=(acts, acts, acts, mats, mats, mats, mats, mats, vec),
        check_vma=False,
    )
```

```python
import functools
import math
from functools import partial

import jax
import jax.numpy as jnp
from jax import lax
from jax.experimental import pallas as pl
from jax.experimental.pallas import tpu as pltpu
from jax.sharding import PartitionSpec as P

D = 1152
HEADS = 16
HD = 72
FF = 4608
EPS = 1e-06
F32 = jnp.float32
BF = jnp.bfloat16
ROOT = HD ** (-0.5)
C2 = ROOT * math.log2(math.e)
BIG = 1e30
IMAGES = 9
NN = (((1,), (0,)), ((), ()))
NT = (((1,), (1,)), ((), ()))
TN = (((0,), (0,)), ((), ()))


def dot(a, b, dims=NN):
    return lax.dot_general(a, b, dims, preferred_element_type=F32)


def lanes(n, w):
    return lax.broadcasted_iota(jnp.int32, (n, w), 1)


def window(first, limit):
    lo = first // 128 * 128
    return lo, min(lo + 256, limit)


def pickers(hpd, parts, limit, out_width, copies):
    firsts = [part * hpd * HD + h * HD for part in parts for h in range(hpd)]
    offsets = jnp.array([f - window(f, limit)[0] for f in firsts], jnp.int32)[:, None, None]
    shape = (len(firsts), 256, out_width)
    r = lax.broadcasted_iota(jnp.int32, shape, 1) - offsets
    c = lax.broadcasted_iota(jnp.int32, shape, 2)
    hit = (r == c) & (c < HD)
    if copies == 2:
        hit = hit | ((r == c - HD) & (c >= HD) & (c < 2 * HD))
    return jnp.where(hit, 1.0, 0.0).astype(BF)


def placer(hpd):
    r = lax.broadcasted_iota(jnp.int32, (hpd * 128, hpd * HD), 0)
    c = lax.broadcasted_iota(jnp.int32, (hpd * 128, hpd * HD), 1)
    hit = (r % 128 < HD) & (c == r // 128 * HD + r % 128)
    return jnp.where(hit, 1.0, 0.0).astype(BF)


def chosen(ref, rows, first, e):
    lo, hi = window(first, ref.shape[2])
    return dot(ref[0, rows, lo:hi], e[: hi - lo])


def split3(v):
    a = v.astype(BF).astype(F32)
    r = v - a
    b = r.astype(BF).astype(F32)
    return a, b, r - b


def query_tags(n, ids):
    lane = lanes(n, 256)
    return jnp.where(lane == 2 * HD + ids, BIG, 0.0)


def key_tags(n, ids):
    lane = lanes(n, 256)
    tag = (lane >= 2 * HD) & (lane < 2 * HD + IMAGES) & (lane != 2 * HD + ids)
    ones = (lane >= 2 * HD + IMAGES) & (lane < 2 * HD + IMAGES + 3)
    return jnp.where(tag, -1.0, jnp.where(ones, 1.0, 0.0))


def in_lanes(n, width, start, parts):
    lane = lanes(n, width)
    out = 0.0
    for t, part in enumerate(parts):
        out = jnp.where(lane == start + t, part, out)
    return out


def aug_query(q, tags):
    q = q * C2
    hi = q.astype(BF).astype(F32)
    out = jnp.where(lanes(q.shape[0], 256) < HD, hi, q - hi)
    return (out + tags).astype(BF)


def once(shape, index):
    return pl.BlockSpec(shape, index, pipeline_mode=pl.Buffered(1))


def forward_kernel(
    hpd, tq, tk, lo_ref, hi_ref, qkv_q, qkv_ref, ids_q, ids_ref, e2_ref, e1_ref, put_ref, o_ref, lse_ref,
    kaug, vaug, s_scr, qa_scr, best_scr, acc_scr,
):
    r = pl.program_id(0)
    i = pl.program_id(1)
    w = hpd * HD
    length = qkv_ref.shape[1]

    @pl.when(i == 0)
    def _():
        def build(j, _):
            rows = pl.ds(pl.multiple_of(j * tk, tk), tk)
            ids = ids_ref[0, rows, :]
            tags = key_tags(tk, ids)
            ones = in_lanes(tk, 128, HD, [1.0])
            for h in range(hpd):
                k = chosen(qkv_ref, rows, w + h * HD, e2_ref[hpd + h])
                kaug[h, rows, :] = (k + tags).astype(BF)
                v = chosen(qkv_ref, rows, 2 * w + h * HD, e1_ref[h])
                vaug[h, rows, :] = (v + ones).astype(BF)
            return 0

        lax.fori_loop(0, length // tk, build, 0)

    lo = lo_ref[r, i]
    hi = hi_ref[r, i]
    ids = ids_q[0]
    lane = lanes(tq, 128)
    tags = query_tags(tq, ids)
    for h in range(hpd):
        qa_scr[h] = aug_query(chosen(qkv_q, slice(None), h * HD, e2_ref[h]), tags)
    best_scr[...] = jnp.full((hpd, tq, 128), -3e38, F32)
    acc_scr[...] = jnp.zeros((hpd, tq, 128), F32)

    def first(j, _):
        rows = pl.ds(pl.multiple_of(j * tk, tk), tk)
        for h in range(hpd):
            s = dot(qa_scr[h], kaug[h, rows, :], NT)
            s_scr[h, :, rows] = s
            best = s[:, 0:128]
            for t in range(1, tk // 128):
                best = jnp.maximum(best, s[:, t * 128 : (t + 1) * 128])
            best_scr[h] = jnp.maximum(best_scr[h], best)
        return 0

    lax.fori_loop(lo, hi, first, 0)
    for h in range(hpd):
        best_scr[h] = jnp.broadcast_to(jnp.max(best_scr[h], axis=1, keepdims=True), (tq, 128))

    def second(j, _):
        rows = pl.ds(pl.multiple_of(j * tk, tk), tk)
        for h in range(hpd):
            top = best_scr[h]
            s = s_scr[h, :, rows]
            p = jnp.concatenate(
                [
                    jnp.exp2(s[:, t * 128 : (t + 1) * 128] - top).astype(BF)
                    for t in range(tk // 128)
                ],
                axis=1,
            )
            acc_scr[h] += dot(p, vaug[h, rows, :])
        return 0

    lax.fori_loop(lo, hi, second, 0)
    outs = []
    lse_all = jnp.zeros((tq, 128), F32)
    for h in range(hpd):
        acc = acc_scr[h]
        total = acc[:, HD : HD + 1]
        o = (acc / total).astype(BF)
        outs.append(jnp.where(lane < HD, o, 0).astype(BF))
        lse_all = jnp.where(lane == h, best_scr[h] + jnp.log2(total), lse_all)
    o_ref[0] = dot(jnp.concatenate(outs, axis=1), put_ref[...]).astype(BF)
    lse_ref[0] = lse_all


def attend_forward(qkv, ids, hpd, tq, tk):
    rows, length, _ = qkv.shape
    w = hpd * HD
    lo, hi = block_ranges(ids, tq, tk)
    column = ids[..., None]
    return pl.pallas_call(
        partial(forward_kernel, hpd, tq, tk),
        grid_spec=pltpu.PrefetchScalarGridSpec(
            num_scalar_prefetch=2,
            grid=(rows, length // tq),
            in_specs=[
                pl.BlockSpec((1, tq, 3 * w), lambda r, i, *_: (r, i, 0)),
                pl.BlockSpec((1, length, 3 * w), lambda r, i, *_: (r, 0, 0)),
                pl.BlockSpec((1, tq, 1), lambda r, i, *_: (r, i, 0)),
                pl.BlockSpec((1, length, 1), lambda r, i, *_: (r, 0, 0)),
                once((2 * hpd, 256, 256), lambda r, i, *_: (0, 0, 0)),
                once((hpd, 256, 128), lambda r, i, *_: (0, 0, 0)),
                once((hpd * 128, w), lambda r, i, *_: (0, 0)),
            ],
            out_specs=[
                pl.BlockSpec((1, tq, w), lambda r, i, *_: (r, i, 0)),
                pl.BlockSpec((1, tq, 128), lambda r, i, *_: (r, i, 0)),
            ],
            scratch_shapes=[
                pltpu.VMEM((hpd, length, 256), BF),
                pltpu.VMEM((hpd, length, 128), BF),
                pltpu.VMEM((hpd, tq, length), F32),
                pltpu.VMEM((hpd, tq, 256), BF),
                pltpu.VMEM((hpd, tq, 128), F32),
                pltpu.VMEM((hpd, tq, 128), F32),
            ],
        ),
        out_shape=[
            jax.ShapeDtypeStruct((rows, length, w), BF),
            jax.ShapeDtypeStruct((rows, length, 128), F32),
        ],
        compiler_params=pltpu.CompilerParams(vmem_limit_bytes=58 << 20),
        cost_estimate=pl.CostEstimate(
            flops=40 * length * length * rows * w,
            bytes_accessed=8 * rows * length * w,
            transcendentals=rows * length * length * hpd,
        ),
        name="attend_forward",
    )(
        lo, hi, qkv, qkv, column, column, pickers(hpd, (0, 1), 3 * w, 256, 2),
        pickers(hpd, (2,), 3 * w, 128, 1), placer(hpd),
    )


def backward_kernel(
    hpd, tq, tk, lo_ref, hi_ref, qkv_ref, g_ref, o_ref, lse_ref, ids_ref, e2_ref, e1_ref, eg_ref, put_ref, dp_ref,
    qaug, qraw, gaug, dq, kaug, vaug, dka, dva,
):
    r = pl.program_id(0)
    w = hpd * HD
    length = qkv_ref.shape[1]
    step = 256

    def build(i, _):
        rows = pl.ds(pl.multiple_of(i * step, step), step)
        ids = ids_ref[0, rows, :]
        lane = lanes(step, 128)
        q_tags = query_tags(step, ids)
        k_tags = key_tags(step, ids)
        ones = in_lanes(step, 128, HD, [1.0] * 3)
        for h in range(hpd):
            lse = lse_ref[0, rows, h : h + 1]
            tags = q_tags + in_lanes(step, 256, 2 * HD + IMAGES, split3(-lse))
            q = chosen(qkv_ref, rows, h * HD, e2_ref[h])
            qaug[h, rows, :] = aug_query(q, tags)
            qraw[h, rows, :] = jnp.where(lane < HD, q[:, :128], 0.0).astype(BF)
            g = chosen(g_ref, rows, h * HD, eg_ref[h])
            o = chosen(o_ref, rows, h * HD, eg_ref[h])
            delta = jnp.sum(g * o, axis=1, keepdims=True)
            gaug[h, rows, :] = (g + in_lanes(step, 128, HD, split3(-delta))).astype(BF)
            k = chosen(qkv_ref, rows, w + h * HD, e2_ref[hpd + h])
            kaug[h, rows, :] = (k + k_tags).astype(BF)
            v = chosen(qkv_ref, rows, 2 * w + h * HD, e1_ref[h])
            vaug[h, rows, :] = (v + ones).astype(BF)
            dq[h, rows, :] = jnp.zeros((step, 128), F32)
        return 0

    lax.fori_loop(0, length // step, build, 0)

    def put(values, n):
        lane = lanes(n, 128)
        parts = [jnp.where(lane < HD, values[h], 0).astype(BF) for h in range(hpd)]
        return dot(jnp.concatenate(parts, axis=1), put_ref[...]).astype(BF)

    def per_key(j, _):
        krows = pl.ds(pl.multiple_of(j * tk, tk), tk)
        dka[...] = jnp.zeros((hpd, tk, 128), F32)
        dva[...] = jnp.zeros((hpd, tk, 128), F32)

        def per_query(i, _):
            rows = pl.ds(pl.multiple_of(i * tq, tq), tq)
            for h in range(hpd):
                ka = kaug[h, krows, :]
                va = vaug[h, krows, :]
                ga = gaug[h, rows, :]
                p = jnp.exp2(dot(ka, qaug[h, rows, :], NT))
                dp = dot(va, ga, NT)
                dva[h] += dot(p.astype(BF), ga)
                ds = (p * dp).astype(BF)
                dka[h] += dot(ds, qraw[h, rows, :])
                dq[h, rows, :] += dot(ds, ka[:, :128], TN)
            return 0

        lax.fori_loop(lo_ref[r, j], hi_ref[r, j], per_query, 0)
        dp_ref[0, krows, w : 2 * w] = put([dka[h] * ROOT for h in range(hpd)], tk)
        dp_ref[0, krows, 2 * w : 3 * w] = put([dva[h] for h in range(hpd)], tk)
        return 0

    lax.fori_loop(0, length // tk, per_key, 0)

    def finish(i, _):
        rows = pl.ds(pl.multiple_of(i * step, step), step)
        dp_ref[0, rows, 0:w] = put([dq[h, rows, :] * ROOT for h in range(hpd)], step)
        return 0

    lax.fori_loop(0, length // step, finish, 0)


def attend_backward(qkv, g, o, lse, ids, hpd, tq, tk):
    rows, length, _ = qkv.shape
    w = hpd * HD
    lo, hi = block_ranges(ids, tk, tq)

    def spec(n):
        return pl.BlockSpec((1, length, n), lambda r, *_: (r, 0, 0))

    return pl.pallas_call(
        partial(backward_kernel, hpd, tq, tk),
        grid_spec=pltpu.PrefetchScalarGridSpec(
            num_scalar_prefetch=2,
            grid=(rows,),
            in_specs=[
                spec(3 * w), spec(w), spec(w), spec(128), spec(1),
                once((2 * hpd, 256, 256), lambda r, *_: (0, 0, 0)),
                once((hpd, 256, 128), lambda r, *_: (0, 0, 0)),
                once((hpd, 256, 128), lambda r, *_: (0, 0, 0)),
                once((hpd * 128, w), lambda r, *_: (0, 0)),
            ],
            out_specs=spec(3 * w),
            scratch_shapes=[
                pltpu.VMEM((hpd, length, 256), BF),
                pltpu.VMEM((hpd, length, 128), BF),
                pltpu.VMEM((hpd, length, 128), BF),
                pltpu.VMEM((hpd, length, 128), F32),
                pltpu.VMEM((hpd, length, 256), BF),
                pltpu.VMEM((hpd, length, 128), BF),
                pltpu.VMEM((hpd, tk, 128), F32),
                pltpu.VMEM((hpd, tk, 128), F32),
            ],
        ),
        out_shape=jax.ShapeDtypeStruct((rows, length, 3 * w), BF),
        compiler_params=pltpu.CompilerParams(vmem_limit_bytes=58 << 20),
        cost_estimate=pl.CostEstimate(
            flops=60 * length * length * rows * w,
            bytes_accessed=18 * rows * length * w,
            transcendentals=rows * length * length * hpd,
        ),
        name="attend_backward",
    )(
        lo, hi, qkv, g, o, lse, ids[..., None], pickers(hpd, (0, 1), 3 * w, 256, 2),
        pickers(hpd, (2,), 3 * w, 128, 1), pickers(hpd, (0,), w, 128, 1), placer(hpd),
    )


def block_ranges(ids, mine, theirs):
    rows, length = ids.shape
    own = ids.reshape(rows, length // mine, mine)
    far = ids.reshape(rows, length // theirs, theirs)
    before = far[:, None, :, -1] < own[:, :, None, 0]
    reached = far[:, None, :, 0] <= own[:, :, None, -1]
    return (
        jnp.sum(before.astype(jnp.int32), axis=-1),
        jnp.sum(reached.astype(jnp.int32), axis=-1),
    )


def params(mib=58):
    return pltpu.CompilerParams(vmem_limit_bytes=mib << 20)


def cost(units, count, moved):
    return pl.CostEstimate(
        flops=int(2 * units * count * D * D), bytes_accessed=int(moved), transcendentals=0
    )


def row_tile(count):
    return 288 if count % 288 == 0 else count


def norm_of(values):
    center = values - jnp.mean(values, axis=-1, keepdims=True)
    spread = jnp.mean(center * center, axis=-1, keepdims=True)
    inverse = lax.rsqrt(spread + EPS)
    return center * inverse, inverse


def norm_back(gradient, n, inverse):
    return (
        gradient
        - jnp.mean(gradient, axis=-1, keepdims=True)
        - n * jnp.mean(gradient * n, axis=-1, keepdims=True)
    ) * inverse


def mix_input_kernel(cond_ref, x_ref, ada_ref, bias_ref, act_ref, input_ref, scale_ref):
    cond = cond_ref[...].astype(F32)
    act = (cond / (1.0 + jnp.exp(-cond))).astype(BF)
    act_ref[...] = act
    parts = [dot(act, ada_ref[i]) for i in range(4)]
    shift = jnp.concatenate(parts[:2], axis=1) + bias_ref[0]
    scale = jnp.concatenate(parts[2:], axis=1) + bias_ref[1]
    normed, _ = norm_of(x_ref[...].astype(F32))
    scale_ref[...] = scale.astype(BF)
    input_ref[...] = (normed * (1.0 + scale) + shift).astype(BF)


def mix_input(cond, x, ada, bias):
    count = cond.shape[0]
    tm = row_tile(count)
    rows = pl.BlockSpec((tm, D), lambda i: (i, 0))
    return pl.pallas_call(
        mix_input_kernel,
        grid=(count // tm,),
        in_specs=[rows, rows, once((4, D, D // 2), lambda i: (0, 0, 0)),
                  once((2, 1, D), lambda i: (0, 0, 0))],
        out_specs=[rows, rows, rows],
        out_shape=[jax.ShapeDtypeStruct((count, D), BF)] * 3,
        compiler_params=params(),
        cost_estimate=cost(2, count, 10 * count * D + 4 * D * D),
        name="mix_input",
    )(cond, x, ada, bias)


def gates_kernel(act_ref, ada_ref, bias_ref, out_ref):
    out_ref[0] = (dot(act_ref[...], ada_ref[0]) + bias_ref[0]).astype(BF)


def feed_gates(act, ada, bias):
    count = act.shape[0]
    return pl.pallas_call(
        gates_kernel,
        grid=(4,),
        in_specs=[once((count, D), lambda i: (0, 0)), pl.BlockSpec((1, D, D), lambda i: (i, 0, 0)),
                  pl.BlockSpec((1, 1, D), lambda i: (i, 0, 0))],
        out_specs=pl.BlockSpec((1, count, D), lambda i: (i, 0, 0)),
        out_shape=jax.ShapeDtypeStruct((4, count, D), BF),
        compiler_params=params(),
        cost_estimate=cost(4, count, 10 * count * D + 8 * D * D),
        name="feed_gates",
    )(act, ada, bias)


def before_feed_kernel(
    attn_ref, x_ref, cot_ref, gates_ref, out_ref, out_bias, mix_ref, middle_ref, input_ref, grad_ref
):
    branch_mix = dot(attn_ref[...], out_ref[...]) + out_bias[...]
    mix_ref[...] = branch_mix.astype(BF)
    middle = x_ref[...].astype(F32) + gates_ref[0].astype(F32) * branch_mix
    middle_ref[...] = middle
    normed, _ = norm_of(middle)
    input_ref[...] = (
        normed * (1.0 + gates_ref[2].astype(F32)) + gates_ref[1].astype(F32)
    ).astype(BF)
    grad_ref[...] = (cot_ref[...].astype(F32) * gates_ref[3].astype(F32)).astype(BF)


def before_feed(attn_out, x, cot, gates, out_mat, out_bias):
    count = x.shape[0]
    tm = row_tile(count)
    rows = pl.BlockSpec((tm, D), lambda i: (i, 0))
    return pl.pallas_call(
        before_feed_kernel,
        grid=(count // tm,),
        in_specs=[rows, rows, rows, pl.BlockSpec((4, tm, D), lambda i: (0, i, 0)),
                  once((D, D), lambda i: (0, 0)), once((1, D), lambda i: (0, 0))],
        out_specs=[rows] * 4,
        out_shape=[
            jax.ShapeDtypeStruct((count, D), BF),
            jax.ShapeDtypeStruct((count, D), F32),
            jax.ShapeDtypeStruct((count, D), BF),
            jax.ShapeDtypeStruct((count, D), BF),
        ],
        compiler_params=params(),
        cost_estimate=cost(1, count, 24 * count * D),
        name="before_feed",
    )(attn_out, x, cot, gates, out_mat, out_bias)


GELU_A = math.sqrt(2.0 / math.pi)
GELU_B = 0.044715


def feed_kernel(
    tm, input_ref, grad_ref, up_ref, down_ref, bias_ref,
    branch_out, shift_out, up_grad_ref, down_grad_ref, bias_grad_ref,
    branch, shift, active, hidden_grad, sem,
):
    t = pl.program_id(0)
    count = input_ref.shape[0]

    @pl.when(t == 0)
    def _():
        branch[...] = jnp.zeros_like(branch)
        shift[...] = jnp.zeros_like(shift)

    total = jnp.zeros((1, active.shape[1]), F32)
    for m in range(count // tm):
        rows = slice(m * tm, (m + 1) * tm)
        h = dot(input_ref[rows, :], up_ref[0]) + bias_ref[0]
        square = h * h
        th = jnp.tanh(GELU_A * h * (1.0 + GELU_B * square))
        half = 0.5 * (1.0 + th)
        act = (h * half).astype(BF)
        slope = half + (0.5 * GELU_A) * h * (1.0 - th * th) * (1.0 + 3.0 * GELU_B * square)
        active[rows, :] = act
        hidden = dot(grad_ref[rows, :], down_ref[0], NT) * slope
        low = hidden.astype(BF)
        hidden_grad[rows, :] = low
        total = total + jnp.sum(low.astype(F32), axis=0, keepdims=True)
        branch[rows, :] += dot(act, down_ref[0])
        shift[rows, :] += dot(low, up_ref[0], NT)
    bias_grad_ref[0] = total
    down_grad_ref[0] = dot(active[...], grad_ref[...], TN).astype(BF)
    up_grad_ref[0] = dot(input_ref[...], hidden_grad[...], TN).astype(BF)

    @pl.when(t == pl.num_programs(0) - 1)
    def _():
        first = pltpu.make_async_copy(branch, branch_out, sem.at[0])
        second = pltpu.make_async_copy(shift, shift_out, sem.at[1])
        first.start()
        second.start()
        first.wait()
        second.wait()


def feed(feed_input, feed_grad, ups, downs, up_bias):
    count = feed_input.shape[0]
    seqs, _, nf = ups.shape
    tm = 384 if count % 384 == 0 else count
    whole = once((count, D), lambda t: (0, 0))
    place = lambda t: (t, 0, 0)
    return pl.pallas_call(
        partial(feed_kernel, tm),
        grid_spec=pltpu.PrefetchScalarGridSpec(
            num_scalar_prefetch=0,
            grid=(seqs,),
            in_specs=[whole, whole, pl.BlockSpec((1, D, nf), place), pl.BlockSpec((1, nf, D), place),
                      pl.BlockSpec((1, 1, nf), place)],
            out_specs=[
                pl.BlockSpec(memory_space=pl.ANY),
                pl.BlockSpec(memory_space=pl.ANY),
                pl.BlockSpec((1, D, nf), place),
                pl.BlockSpec((1, nf, D), place),
                pl.BlockSpec((1, 1, nf), place),
            ],
            scratch_shapes=[
                pltpu.VMEM((count, D), F32),
                pltpu.VMEM((count, D), F32),
                pltpu.VMEM((count, nf), BF),
                pltpu.VMEM((count, nf), BF),
                pltpu.SemaphoreType.DMA((2,)),
            ],
        ),
        out_shape=[
            jax.ShapeDtypeStruct((count, D), F32),
            jax.ShapeDtypeStruct((count, D), F32),
            jax.ShapeDtypeStruct((seqs, D, nf), BF),
            jax.ShapeDtypeStruct((seqs, nf, D), BF),
            jax.ShapeDtypeStruct((seqs, 1, nf), F32),
        ],
        compiler_params=params(62),
        cost_estimate=cost(24 * FF // (4 * D), count, 16 * count * D + 8 * FF * D),
        name="feed",
    )(feed_input, feed_grad, ups, downs, up_bias)


def after_feed_kernel(
    first, branch_ref, shift_ref, middle_ref, gates_ref, mix_ref, cot_ref, out_ref, bias_ref,
    block_ref, late_ref, mix_grad_ref, attn_grad_ref, middle_grad_ref,
):
    cot = cot_ref[...].astype(F32)
    middle = middle_ref[...]
    branch = branch_ref[...] + bias_ref[...]
    block_ref[...] = (middle + gates_ref[3].astype(F32) * branch).astype(BF)
    late_ref[3] = (cot * branch).astype(BF)
    shift = shift_ref[...]
    late_ref[1] = shift.astype(BF)
    normed, inverse = norm_of(middle)
    late_ref[2] = (shift * normed).astype(BF)
    middle_grad = cot + norm_back(shift * (1.0 + gates_ref[2].astype(F32)), normed, inverse)
    middle_grad_ref[...] = middle_grad
    late_ref[0] = (middle_grad * mix_ref[...].astype(F32)).astype(BF)
    mix_grad = (middle_grad * gates_ref[0].astype(F32)).astype(BF)
    mix_grad_ref[...] = mix_grad
    attn_grad = dot(mix_grad, out_ref[...], NT).astype(BF)
    w = attn_grad_ref.shape[3]
    for s in range(attn_grad_ref.shape[0]):
        attn_grad_ref[s, 0] = attn_grad[:, s * w : (s + 1) * w]


def after_feed(first, seqs, own, branch, shift, middle, gates, mix, cot, out_mat, down_bias):
    count = branch.shape[0]
    tm = 288 if own % 288 == 0 else own
    steps = own // tm
    rows = pl.BlockSpec((tm, D), lambda i, f: (i, 0))
    return pl.pallas_call(
        after_feed_kernel,
        grid_spec=pltpu.PrefetchScalarGridSpec(
            num_scalar_prefetch=1,
            grid=(count // tm,),
            in_specs=[rows, rows, rows, pl.BlockSpec((4, tm, D), lambda i, f: (0, i, 0)), rows, rows,
                      once((D, D), lambda i, f: (0, 0)), once((1, D), lambda i, f: (0, 0))],
            out_specs=[
                rows, pl.BlockSpec((4, tm, D), lambda i, f: (0, i, 0)), rows,
                pl.BlockSpec(
                    (seqs, 1, tm, D // seqs),
                    lambda i, f: (0, (i // steps + f[0]) % 2, i % steps, 0),
                ),
                rows,
            ],
        ),
        out_shape=[
            jax.ShapeDtypeStruct((count, D), BF),
            jax.ShapeDtypeStruct((4, count, D), BF),
            jax.ShapeDtypeStruct((count, D), BF),
            jax.ShapeDtypeStruct((seqs, count // own, own, D // seqs), BF),
            jax.ShapeDtypeStruct((count, D), F32),
        ],
        compiler_params=params(),
        cost_estimate=cost(1, count, 44 * count * D),
        name="after_feed",
    )(first, branch, shift, middle, gates, mix, cot, out_mat, down_bias)


def late_products_kernel(turns, order, act_ref, grad_ref, give_ref, keep_ref, sum_ref):
    grad = grad_ref[0]
    out = dot(act_ref[...], grad, TN).astype(BF)
    t = pl.program_id(0)

    @pl.when(t < turns)
    def _():
        give_ref[0] = out

    @pl.when(t >= turns)
    def _():
        keep_ref[0] = out

    sum_ref[0] = jnp.sum(grad.astype(F32), axis=0, keepdims=True)


def late_products(order, act, grads):
    parts, count, _ = grads.shape
    turns = parts // 2
    return pl.pallas_call(
        partial(late_products_kernel, turns),
        grid_spec=pltpu.PrefetchScalarGridSpec(
            num_scalar_prefetch=1,
            grid=(parts,),
            in_specs=[once((count, D), lambda t, o: (0, 0)),
                      pl.BlockSpec((1, count, D), lambda t, o: (o[t], 0, 0))],
            out_specs=[pl.BlockSpec((1, D, D), lambda t, o: (jnp.minimum(t, turns - 1), 0, 0)),
                       pl.BlockSpec((1, D, D), lambda t, o: (jnp.maximum(t - turns, 0), 0, 0)),
                       pl.BlockSpec((1, 1, D), lambda t, o: (o[t], 0, 0))],
        ),
        out_shape=[
            jax.ShapeDtypeStruct((turns, D, D), BF),
            jax.ShapeDtypeStruct((turns, D, D), BF),
            jax.ShapeDtypeStruct((parts, 1, D), F32),
        ],
        compiler_params=params(),
        cost_estimate=cost(parts, count, 2 * (parts + 1) * count * D + 2 * parts * D * D),
        name="late_products",
    )(order, act, grads)


def early_products_kernel(act_ref, grad_ref, out_ref, sum_ref):
    grad = grad_ref[0]
    out = dot(act_ref[...], grad, TN).astype(BF)
    out_ref[0] = out[:, : D // 2]
    out_ref[1] = out[:, D // 2 :]
    sum_ref[0] = jnp.sum(grad.astype(F32), axis=0, keepdims=True)


def early_products(act, grads):
    parts, count, _ = grads.shape
    return pl.pallas_call(
        early_products_kernel,
        grid=(parts,),
        in_specs=[once((count, D), lambda t: (0, 0)),
                  pl.BlockSpec((1, count, D), lambda t: (t, 0, 0))],
        out_specs=[pl.BlockSpec((2, D, D // 2), lambda t: (t, 0, 0)),
                   pl.BlockSpec((1, 1, D), lambda t: (t, 0, 0))],
        out_shape=[
            jax.ShapeDtypeStruct((2 * parts, D, D // 2), BF),
            jax.ShapeDtypeStruct((parts, 1, D), F32),
        ],
        compiler_params=params(),
        cost_estimate=cost(parts, count, 2 * (parts + 1) * count * D + 2 * parts * D * D),
        name="early_products",
    )(act, grads)


def head_products_kernel(blocks, places, *refs):
    own = refs[0].shape[0]
    grad_ref, out_ref = refs[blocks], refs[-1]
    for t in range(blocks):
        rows = pl.ds(pl.multiple_of(places[t] * own, own), own)
        part = dot(refs[t][...], grad_ref[rows, :], TN)
        if t == 0:
            out_ref[...] = part if len(refs) == blocks + 2 else part + refs[blocks + 1][...]
        else:
            out_ref[...] += part


def head_products(places, blocks, grad, *start):
    n = grad.shape[1]
    vmem = pl.BlockSpec(memory_space=pltpu.VMEM)
    return pl.pallas_call(
        partial(head_products_kernel, len(blocks)),
        grid_spec=pltpu.PrefetchScalarGridSpec(
            num_scalar_prefetch=1,
            grid=(),
            in_specs=[vmem] * (len(blocks) + 1 + len(start)),
            out_specs=vmem,
        ),
        out_shape=jax.ShapeDtypeStruct((D, n), F32),
        compiler_params=params(),
        cost_estimate=pl.CostEstimate(
            flops=2 * grad.shape[0] * D * n, bytes_accessed=2 * grad.size + 8 * D * n, transcendentals=0
        ),
        name="head_products",
    )(places, *blocks, grad, *start)


def after_mix_kernel(grad_ref, x_ref, scale_ref, middle_grad_ref, early_ref, tokens_grad_ref):
    grad = grad_ref[...].astype(F32)
    normed, inverse = norm_of(x_ref[...].astype(F32))
    early_ref[0] = grad.astype(BF)
    early_ref[1] = (grad * normed).astype(BF)
    back = norm_back(grad * (1.0 + scale_ref[...].astype(F32)), normed, inverse)
    tokens_grad_ref[...] = middle_grad_ref[...] + back


def after_mix(grad, x, scale, middle_grad):
    count = x.shape[0]
    tm = row_tile(count)
    rows = pl.BlockSpec((tm, D), lambda i: (i, 0))
    return pl.pallas_call(
        after_mix_kernel,
        grid=(count // tm,),
        in_specs=[rows] * 4,
        out_specs=[pl.BlockSpec((2, tm, D), lambda i: (0, i, 0)), rows],
        out_shape=[
            jax.ShapeDtypeStruct((2, count, D), BF),
            jax.ShapeDtypeStruct((count, D), F32),
        ],
        compiler_params=params(),
        cost_estimate=cost(0, count, 18 * count * D),
        name="after_mix",
    )(grad, x, scale, middle_grad)


def to_condition_kernel(parts, last, grads_ref, ada_ref, *refs):
    out_ref, total = refs[-2:]
    t = pl.program_id(1)
    n = ada_ref.shape[2]
    part = sum(
        dot(grads_ref[0][:, k * n : (k + 1) * n], ada_ref[k], NT) for k in range(ada_ref.shape[0])
    )

    @pl.when(t == 0)
    def _():
        total[...] = part + refs[0][...] if last else part

    @pl.when(t > 0)
    def _():
        total[...] += part

    @pl.when(t == parts - 1)
    def _():
        if last:
            cond = refs[1][...].astype(F32)
            gate = 1.0 / (1.0 + jnp.exp(-cond))
            out_ref[...] = total[...] * (gate * (1.0 + cond * (1.0 - gate)))
        else:
            out_ref[...] = total[...]


def to_condition(grads, ada, *rest):
    parts, count, _ = grads.shape
    tm = count // 2 if count % 32 == 0 else count
    rows = pl.BlockSpec((tm, D), lambda m, t: (m, 0))
    return pl.pallas_call(
        partial(to_condition_kernel, parts, len(rest) > 0),
        grid=(count // tm, parts),
        in_specs=[pl.BlockSpec((1, tm, D), lambda m, t: (t, m, 0)),
                  pl.BlockSpec((ada.shape[0] // parts, D, ada.shape[2]), lambda m, t: (t, 0, 0))]
        + [rows] * len(rest),
        out_specs=rows,
        scratch_shapes=[pltpu.VMEM((tm, D), F32)],
        out_shape=jax.ShapeDtypeStruct((count, D), F32),
        compiler_params=params(),
        cost_estimate=cost(parts, count, 2 * parts * count * D + 12 * count * D),
        name="to_condition",
    )(grads, ada, *rest)


class Places:
    def __init__(self, packs, seqs):
        self.packs, self.seqs = packs, seqs
        self.rings, self.sides = packs // 2, seqs // 2
        self.pack = lax.axis_index("pack")
        self.seq = lax.axis_index("seq")
        self.a, self.b = self.pack // 2, self.pack % 2
        self.y, self.c = self.seq // 2, self.seq % 2

    def ring(self, value, k):
        n = self.rings
        pairs = [(a * 2 + b, ((a + k) % n) * 2 + b) for a in range(n) for b in range(2)]
        return lax.ppermute(value, "pack", pairs)

    def cross(self, value):
        return lax.ppermute(value, "pack", [(p, p ^ 1) for p in range(self.packs)])

    def side(self, value, k):
        n = self.sides
        pairs = [(y * 2 + c, ((y + k) % n) * 2 + c) for y in range(n) for c in range(2)]
        return lax.ppermute(value, "seq", pairs)

    def core(self, value):
        return lax.ppermute(value, "seq", [(s, s ^ 1) for s in range(self.seqs)])

    def gather_by(self, shard, members):
        groups = [[p * self.seqs + s for s in group for p in range(self.packs)] for group in members]
        out = lax.all_gather(
            shard, ("pack", "seq"), axis=0, tiled=True, axis_index_groups=groups
        )
        return out.reshape((len(members[0]), self.packs) + shard.shape)

    def gather_seq(self, value):
        whole = jnp.zeros((self.seqs,) + value.shape, value.dtype)
        rest = (0,) * value.ndim
        for k in range(self.sides):
            block = value if k == 0 else self.side(value, k)
            side = (self.y - k + self.sides) % self.sides
            whole = lax.dynamic_update_slice(whole, block[None], (side * 2 + self.c,) + rest)
            whole = lax.dynamic_update_slice(
                whole, self.core(block)[None], (side * 2 + 1 - self.c,) + rest
            )
        return whole

    def two(self, own, other):
        return jnp.where(self.c == 0, own, other), jnp.where(self.c == 0, other, own)

    def ring_blocks(self, value):
        return [value if k == 0 else self.ring(value, k) for k in range(self.rings)]

    def ring_join(self, blocks):
        rest = (0,) * blocks[0].ndim
        part = jnp.zeros((self.rings,) + blocks[0].shape, blocks[0].dtype)
        for k, block in enumerate(blocks):
            place = (self.a - k + self.rings) % self.rings
            part = lax.dynamic_update_slice(part, block[None], (place,) + rest)
        return part

    def cross_join(self, part, other):
        rest = (0,) * (part.ndim - 1)
        whole = jnp.zeros((self.rings, 2) + part.shape[1:], part.dtype)
        whole = lax.dynamic_update_slice(whole, part[:, None], (0, self.b) + rest)
        whole = lax.dynamic_update_slice(whole, other[:, None], (0, 1 - self.b) + rest)
        return whole.reshape((self.packs,) + part.shape[1:])

    def list_seq(self, value):
        if self.seqs != 4:
            whole = self.gather_seq(value)
            return [whole[s] for s in range(self.seqs)]
        far = self.side(value, 1)
        near = self.two(value, self.core(value))
        away = self.two(far, self.core(far))
        pairs = [jnp.where(self.y == y, near[c], away[c]) for y in range(2) for c in range(2)]
        return pairs

    def gather_pack(self, value):
        part = self.ring_join(self.ring_blocks(value))
        return self.cross_join(part, self.cross(part))

    def scatter_all(self, whole):
        r, n = whole.shape[2:]
        order = [[p * self.seqs + s for s in range(self.seqs) for p in range(self.packs)]]
        return lax.psum_scatter(
            whole.reshape(-1, n), ("pack", "seq"), scatter_dimension=0, tiled=True,
            axis_index_groups=order,
        )

    def reduce_core(self, pieces):
        give = lax.dynamic_index_in_dim(pieces, 1 - self.c, 1, False)
        keep = lax.dynamic_index_in_dim(pieces, self.c, 1, False)
        return add(keep, self.core(give), kind=pieces.dtype)

    def reduce_cross(self, whole):
        split = whole.reshape((whole.shape[0], self.rings, 2) + whole.shape[2:])
        give = lax.dynamic_index_in_dim(split, 1 - self.b, 2, False)
        keep = lax.dynamic_index_in_dim(split, self.b, 2, False)
        return add(keep, self.cross(give), kind=whole.dtype)

    def reduce_ring(self, part):
        groups = [[a * 2 + b for a in range(self.rings)] for b in range(2)]
        parts = lax.all_to_all(part, "pack", 1, 1, axis_index_groups=groups, tiled=True)
        return jnp.sum(parts.astype(F32), axis=1)

    def reduce_pack(self, whole):
        return self.reduce_ring(self.reduce_cross(whole[None]))[0]

    def reduce_side(self, pieces):
        terms = [lax.dynamic_index_in_dim(pieces, self.y, 0, False)]
        for k in range(1, self.sides):
            block = lax.dynamic_index_in_dim(pieces, (self.y + k) % self.sides, 0, False)
            terms.append(self.side(block, k))
        return add(*terms, kind=pieces.dtype)

def after(value, first):
    return lax.optimization_barrier((value, first))


def add(*terms, kind=BF):
    total = terms[0].astype(F32)
    for term in terms[1:]:
        total = total + term.astype(F32)
    return total.astype(kind)


def token_sum(gradient):
    return jnp.sum(gradient.astype(F32), axis=0)


def per_device(packs, seqs, tokens, condition, image_ids, ada_weight, attn_weight, out_weight,
               up_weight, down_weight, biases, cotangent):
    at = Places(packs, seqs)
    rows, own = image_ids.shape
    length = own * seqs
    count = rows * own
    hpd = HEADS // seqs
    w = hpd * HD
    r = D // packs
    rf = FF // packs
    n2 = 4 * D // seqs
    nf = FF // seqs

    bias_len = biases.shape[0]
    padded = -(-bias_len // 512) * 512
    half = D // 2
    ids = at.gather_seq(image_ids).transpose(1, 0, 2).reshape(rows, length)
    first = jnp.where(ids[0, length - 1] == 0, 0, 1)
    def in_order(values):
        return jnp.where(
            first == 0, jnp.concatenate(values, axis=0), jnp.concatenate(values[::-1], axis=0)
        )

    cut, nd = attn_weight.shape[1], down_weight.shape[1]
    skip = cut + out_weight.shape[1]
    rq = rf // seqs

    def side_by_side():
        downs = [down_weight[s * rq : (s + 1) * rq] for s in range(seqs)] if rq == r else []
        return jnp.concatenate([attn_weight, out_weight] + downs, axis=1)

    if seqs == 4:
        left, right = ada_weight[:, :D], ada_weight[:, D:]
        head, tail = ada_weight[:, :half], ada_weight[:, half:]
        side_got = lax.ppermute(jnp.where(at.seq == 0, right, head), "seq", [(0, 2), (1, 3)])
        core_got = lax.ppermute(
            jnp.where(at.seq == 0, jnp.roll(left, half, axis=1), jnp.where(at.seq == 1, tail, left)),
            "seq", [(0, 1), (1, 0), (3, 2)],
        )
        shard1 = jnp.where(at.seq == 0, head, jnp.where(at.seq == 1, core_got[:, :half], side_got))
        shard1, biases, attn_weight, out_weight, down_weight, ada_weight = lax.optimization_barrier(
            (shard1, biases, attn_weight, out_weight, down_weight, ada_weight)
        )
        far_got = lax.ppermute(ada_weight[:, :D], "seq", [(2, 1)])
        merged = jnp.concatenate([ada_weight[:, D:], core_got[:, :half]], axis=1)
        shard2 = jnp.where(
            at.seq == 0, core_got,
            jnp.where(at.seq == 1, far_got, jnp.where(at.seq == 2, merged, ada_weight[:, half:])),
        )
        both = at.list_seq(side_by_side())
    else:
        both = at.list_seq(side_by_side())
        ada_rows = jnp.concatenate(at.list_seq(ada_weight), axis=1)
        shard1 = lax.dynamic_slice_in_dim(ada_rows, at.seq * (n2 // 2), n2 // 2, 1)
        shard2 = lax.dynamic_slice_in_dim(ada_rows, 2 * D + at.seq * n2, n2, 1)
    attn_rows = jnp.concatenate([block[:, :cut] for block in both], axis=1)
    out_rows = jnp.concatenate([block[:, cut:skip] for block in both], axis=1)
    every = [range(seqs)]
    ada1 = at.gather_by(shard1, every)
    ada1 = ada1.reshape(4, seqs // 4, D, n2 // 2).transpose(0, 2, 1, 3).reshape(4, D, half)
    mine = lax.dynamic_slice_in_dim(attn_rows.reshape(r, 3, seqs, w), at.seq, 1, 2)
    wide = 640
    out_half = jnp.where(at.c == 0, out_rows[:, :wide], out_rows[:, D - wide :])
    packed = jnp.concatenate([out_half, mine.reshape(r, 3 * w)], axis=1)
    lined = jnp.pad(biases, (0, padded - bias_len)).reshape(-1, 128)
    offsets = at.gather_pack(at.gather_seq(lined)).reshape(packs, seqs, padded)
    offsets = offsets[:, :, :bias_len].reshape(-1)

    ring_blocks = at.ring_blocks(packed)
    shard2, offsets, ids, first, ring_blocks = lax.optimization_barrier(
        (shard2, offsets, ids, first, ring_blocks)
    )
    ada2 = at.gather_by(shard2, every)
    ada2 = ada2.reshape(4, seqs // 4, D, n2).transpose(0, 2, 1, 3).reshape(4, D, D)
    if rq == r:
        down_rows = jnp.concatenate(
            [
                sum(
                    jnp.where(at.seq == s, block[:, skip + s * nd : skip + (s + 1) * nd], 0)
                    for s in range(seqs)
                )
                for block in both
            ],
            axis=1,
        ).astype(BF)
    else:
        down_parts = lax.all_to_all(down_weight.reshape(seqs, rq, nd), "seq", 0, 0, tiled=True)
        down_rows = jnp.concatenate([down_parts[s] for s in range(seqs)], axis=1)
    down_rows, up_weight, ada1 = lax.optimization_barrier((down_rows, up_weight, ada1))
    down_mat = lax.all_gather(down_rows, ("pack", "seq"), axis=0, tiled=True)
    down_mats = down_mat.reshape(seqs, nf, D)
    up_mats = at.gather_by(up_weight, every).reshape(seqs, D, nf)

    x = tokens.reshape(count, D).astype(F32)
    ring_part = at.ring_join(ring_blocks)
    cond_act, attn_input, scale_mix = mix_input(
        condition.reshape(count, D), tokens.reshape(count, D), ada1,
        offsets[: 2 * D].astype(F32).reshape(2, 1, D),
    )
    attn_input = attn_input.reshape(rows, own, D)
    query_offset = offsets[6 * D : 7 * D]
    value_offset = offsets[7 * D : 8 * D]
    out_offset = offsets[8 * D : 9 * D]
    up_offset = offsets[9 * D : 9 * D + FF]
    down_offset = offsets[9 * D + FF :]

    head_offset = jnp.concatenate(
        [
            lax.dynamic_slice_in_dim(query_offset, at.seq * w, w),
            jnp.zeros((w,), BF),
            lax.dynamic_slice_in_dim(value_offset, at.seq * w, w),
        ]
    )

    row_order = [first, 1 - first]
    starts = [lax.dynamic_index_in_dim(attn_input, row, 0, False) for row in row_order]
    ring_other = at.cross(ring_part)

    inputs, qkvs, heads, lses, outs = [], [], [], [], []
    id_rows = [lax.dynamic_slice_in_dim(ids, row, 1, 0) for row in row_order]
    for row in range(rows):
        start = starts[row]
        blocks = []
        for k in range(at.sides):
            block = start if k == 0 else at.side(start, k)
            if k and row == 0:
                ring_other, block = after(ring_other, block)
            if k and row + 1 < rows:
                starts[row + 1], block = after(starts[row + 1], block)
            if k and row:
                block, heads[row - 1] = after(block, heads[row - 1])
            side = (at.y - k + at.sides) % at.sides
            blocks += [(side * 2 + at.c, block), (side * 2 + 1 - at.c, at.core(block))]
        inputs.append(blocks)
        if row == 0:
            packed = at.cross_join(ring_part, ring_other).reshape(D, wide + 3 * w)
            out_own, attn_mat = packed[:, :wide], packed[:, wide:]
        qkv = jnp.zeros((seqs, own, 3 * w), BF)
        for place, block in blocks:
            part = (dot(block, attn_mat) + head_offset).astype(BF)
            qkv = lax.dynamic_update_slice(qkv, part[None], (place, 0, 0))
        qkvs.append(qkv.reshape(1, length, 3 * w))
        head, lse = attend_forward(qkvs[row], id_rows[row], hpd, 256 if row else 768, 768)
        heads.append(head)
        lses.append(lse)
    for row in range(rows):
        outs.append(lax.all_to_all(heads[row][0], "seq", 0, 1, tiled=True))
    out_left, out_right = at.two(out_own, at.core(out_own))
    out_mat = jnp.concatenate([out_left, out_right[:, 2 * wide - D :]], axis=1)

    def line(values, parts):
        return values.astype(F32).reshape(parts + (1, -1))

    gate_act, heads[-1] = after(cond_act, heads[-1])
    gates = feed_gates(gate_act, ada2, line(offsets[2 * D : 6 * D], (4,)))
    gates, outs[-1] = after(gates, outs[-1])
    attn_out = in_order(outs)
    branch_mix, middle, feed_input, feed_out_grad = before_feed(
        attn_out, tokens.reshape(count, D), cotangent.reshape(count, D), gates, out_mat,
        line(out_offset, ()),
    )
    branch_feed, shift_sum, up_whole, down_whole, up_sums = feed(
        feed_input, feed_out_grad, up_mats, down_mats, line(up_offset, (seqs,))
    )
    block_out, late, mix_out_grad, attn_out_grad, middle_grad = after_feed(
        first.astype(jnp.int32).reshape(1), seqs, own, branch_feed, shift_sum, middle, gates, branch_mix, cotangent.reshape(count, D), out_mat,
        line(down_offset, ()),
    )

    down_part = lax.psum_scatter(
        down_whole.reshape(FF, D), ("pack", "seq"), scatter_dimension=0, tiled=True
    )
    up_grad = at.scatter_all(up_whole.reshape(seqs, packs, r, nf)).astype(F32)
    both_heads = lax.all_to_all(attn_out_grad, "seq", 0, 0, tiled=True)
    grad_heads = [both_heads[:, row].reshape(length, w) for row in range(rows)]
    out_whole = dot(attn_out, mix_out_grad, TN).astype(BF).reshape(packs, 2, r // 2, D)
    if seqs == 4:
        turn = jnp.stack([y * 2 + core for core in (1 - at.c, at.c) for y in range(2)])
        late_give, late_keep, late_sums = late_products(turn.astype(jnp.int32), cond_act, late)
        late_core = add(late_keep, at.core(late_give)).reshape(2, packs, r, D)
        late_pair = at.reduce_cross(late_core)
        out_core = at.reduce_core(out_whole)
    else:
        late_give, late_keep, late_sums = late_products(jnp.arange(4, dtype=jnp.int32), cond_act, late)
        late_whole = jnp.concatenate([late_give, late_keep])
        late_whole = late_whole.reshape(4, packs, r, seqs // 4, n2).transpose(0, 3, 1, 2, 4)
        ada_late = at.scatter_all(late_whole.reshape(seqs, packs, r, n2))
        out_core = at.reduce_core(out_whole)
    grad_heads[0], out_core = after(grad_heads[0], out_core)
    out_pair = at.reduce_cross(out_core[None])
    input_grads, flat_grads = [], []
    for row in range(rows):
        if row == 1:
            grad_heads[1], flat_grads[0] = after(grad_heads[1], flat_grads[0])
        grad = attend_backward(
            qkvs[row], grad_heads[row][None], heads[row], lses[row], id_rows[row], hpd, 256 if row else 768, 768
        )[0]
        if row == 0:
            grad, down_part = after(grad, down_part)
        else:
            grad, input_grads[0] = after(grad, input_grads[0])
        part = dot(grad, attn_mat, NT).astype(BF).reshape(at.sides, 2, own, D)
        input_grads.append(at.reduce_side(at.reduce_core(part)))
        if row == 1:
            grad, out_pair = after(grad, out_pair)
            out_ring = at.reduce_ring(out_pair)[0].astype(BF)
            if seqs == 4:
                grad, late_pair = after(grad, late_pair)
                late_ring = at.reduce_ring(late_pair).astype(BF)
        flat_grads.append(grad)
        places = jnp.stack([place for place, _ in inputs[row]]).astype(jnp.int32)
        attn_whole = head_products(
            places, [block for _, block in inputs[row]], grad, *([attn_whole] if row else [])
        )
    late, flat_grads = after(late, flat_grads)
    cond_part = to_condition(late, ada2)
    input_grad, up_grad = after(in_order(input_grads), up_grad)
    out_side = at.reduce_side(out_ring.reshape(r // 2, at.sides, -1).transpose(1, 0, 2))
    out_side = out_side.reshape(r // 2, 2, -1).transpose(1, 0, 2)
    out_far = at.core(lax.dynamic_index_in_dim(out_side, 1 - at.c, 0, False))
    out_near = lax.dynamic_index_in_dim(out_side, at.c, 0, False)
    out_grad = jnp.concatenate(at.two(out_near, out_far)).astype(F32)
    if seqs == 4:
        ada_late = at.reduce_side(late_ring)
    attn_pair = at.reduce_cross(attn_whole.astype(BF).reshape(1, packs, r, 3 * w))
    early, tokens_grad = after_mix(input_grad, tokens.reshape(count, D), scale_mix, middle_grad)
    early_whole, early_sums = early_products(cond_act, early)
    early_whole, attn_pair = after(early_whole, attn_pair)
    attn_part = at.reduce_ring(attn_pair)[0].astype(BF)
    early_whole = early_whole.reshape(4, packs, r, seqs // 4, n2 // 2).transpose(0, 3, 1, 2, 4)
    early_got = at.scatter_all(early_whole.reshape(seqs, packs, r, n2 // 2))
    condition_grad = to_condition(early, ada1, cond_part, condition.reshape(count, D))
    early_got, condition_grad = after(early_got, condition_grad)

    def own_columns(whole):
        n = whole.shape[1] // seqs
        return lax.dynamic_slice_in_dim(whole, at.seq * n, n, 1).astype(F32)

    if seqs == 4:
        early_core = lax.ppermute(early_got, "seq", [(1, 0)])
        early_half = lax.ppermute(early_got, "seq", [(2, 0), (3, 1)])
        swapped = lax.ppermute(ada_late, "seq", [(0, 1), (1, 2)])
        late_half = lax.ppermute(ada_late[:, half:], "seq", [(2, 3)])
        whole_part = jnp.where(
            at.seq == 0, jnp.concatenate([early_got, early_core], axis=1),
            jnp.where(at.seq == 3, ada_late, swapped)
        )
        half_part = jnp.where(at.seq == 2, ada_late[:, :half], early_half + late_half)
        ada_grad = jnp.where(
            at.c == 0,
            jnp.concatenate([whole_part, half_part], axis=1),
            jnp.concatenate([half_part, whole_part], axis=1),
        ).astype(F32)
    else:
        early_all = jnp.concatenate(at.list_seq(early_got), axis=1)
        late_all = at.gather_seq(ada_late).transpose(1, 0, 2).reshape(r, 4 * D)
        ada_grad = own_columns(jnp.concatenate([early_all, late_all], axis=1))
    attn_all = at.gather_seq(attn_part).reshape(seqs, r, 3, w).transpose(1, 2, 0, 3).reshape(r, 3 * D)

    down_parts = at.list_seq(down_part)
    down_grad = jnp.concatenate(
        [
            sum(
                jnp.where(at.seq == s, block[:, s * nd : (s + 1) * nd].astype(F32), 0.0)
                for s in range(seqs)
            )
            for block in down_parts
        ]
    )

    head_sum = sum(token_sum(g) for g in flat_grads).reshape(3, w)
    zero = jnp.zeros((D,), F32)
    head_sums = [
        lax.dynamic_update_slice_in_dim(zero, head_sum[i], at.seq * w, 0) for i in (0, 2)
    ]
    bias_whole = jnp.concatenate(
        [early_sums.reshape(-1), late_sums.reshape(-1)]
        + head_sums
        + [token_sum(mix_out_grad)]
        + [up_sums.reshape(-1)]
        + [token_sum(feed_out_grad)]
    )
    bias_whole = jnp.pad(bias_whole.reshape(packs, seqs, bias_len), ((0, 0), (0, 0), (0, padded - bias_len)))
    bias_whole = bias_whole.transpose(1, 0, 2).reshape(at.sides, 2, packs, padded // 128, 128)
    bias_part = at.reduce_side(at.reduce_core(bias_whole))
    bias_grad = at.reduce_pack(bias_part).reshape(-1)[:bias_len]
    return (
        block_out.reshape(tokens.shape),
        tokens_grad.reshape(tokens.shape),
        condition_grad.reshape(tokens.shape),
        ada_grad,
        own_columns(attn_all),
        out_grad,
        up_grad,
        down_grad,
        bias_grad,
    )


def solution(mesh):
    acts = P("pack", "seq", None)
    mats = P("pack", "seq")
    vec = P(("pack", "seq"))
    return jax.shard_map(
        partial(per_device, mesh.shape["pack"], mesh.shape["seq"]),
        mesh=mesh,
        in_specs=(acts, acts, mats, mats, mats, mats, mats, mats, vec, acts),
        out_specs=(acts, acts, acts, mats, mats, mats, mats, mats, vec),
        check_vma=False,
    )
```
